128 devices in a mesh: row: 4 (over x), col: 16 (over y, z_lo, core), dp: 2 (over z_hi).
Axes of the slice: x: 4, y: 4, z: 4 (z_hi: 2, z_lo: 2; z = z_hi * 2 + z_lo), core: 2. Of those that a mesh axis runs over, the one named last changes fastest.
Arguments:
- gradients: bfloat16 [2, 2560, 14336], P('dp', 'row', 'col'), may hold values from -6 to 6
- left_basis: bfloat16 [2560, 2560], P('col', 'row'), may hold values from -0.125 to 0.125
- right_basis: bfloat16 [14336, 14336], P('col', ('row', 'dp')), may hold values from -0.046875 to 0.046875
- first_moment: float32 [2560, 14336], P('col', ('row', 'dp')), may hold values from -1.8 to 1.8
- second_moment: float32 [2560, 14336], P('col', ('row', 'dp')), may hold values from 0.02 to 0.5
- omega_left: bfloat16 [2560, 128], replicated, may hold values from -0.125 to 0.125
- omega_right: bfloat16 [14336, 128], P('col'), may hold values from -0.046875 to 0.046875
- sketch_left: float32 [2560, 128], P(('row', 'col', 'dp')), may hold values from -6 to 6
- sketch_right: float32 [14336, 128], P('col'), may hold values from -6 to 6
Outputs:
- update: bfloat16 [2560, 14336], P(('row', 'dp'), 'col')
- first_new: float32 [2560, 14336], P('col', ('row', 'dp'))
- second_new: float32 [2560, 14336], P('col', ('row', 'dp'))
- left_new: float32 [2560, 128], P(('row', 'col', 'dp'))
- right_new: float32 [14336, 128], P('col')
The draws below stay inside these ranges and needn't reach their ends.
All inputs are finite; a program needn't handle non-finite values.
Results may differ from the reference program's by a relative error of at most 0.027.
Values may be sent and summed in bfloat16 or wider, within the bound.
No kernel may reach another device: no remote copies, remote signals or barrier semaphores. Data moves between devices by JAX's collectives and lax.ppermute only.
A program may use at most 128 MiB of HBM per device.

```python
import math
import jax
import jax.numpy as jnp
from jax import lax

D = 2560
F = 14336
K = 128
N_ROW = 4
N_COL = 16
N_DP = 2


def levels(own_key, extent, cuts, least, largest):
    def one(dim, blocks):
        steps = jax.random.uniform(jax.random.fold_in(jax.random.fold_in(own_key, 6), dim), (blocks,), jnp.float32, least / len(cuts), largest / len(cuts))
        return jnp.repeat(jnp.exp(steps), extent[dim] // blocks).reshape((-1,) + (1,) * (len(extent) - dim - 1))

    factor_of = one(*cuts[0])
    for cut in cuts[1:]:
        factor_of = factor_of * one(*cut)
    return factor_of


def normal_values(key, shape, width, reach, cuts=(), held_as=jnp.bfloat16):
    array = jax.random.normal(key, shape, jnp.float32) * width
    if len(cuts) > 0:
        array = levels(key, shape, cuts, -0.22, 0.18) * array
    return jnp.clip(array, min=-reach, max=reach).astype(held_as)


def setup_inputs(seed: int = 0) -> dict:
    seeds = jax.random.split(jax.random.key(seed), 10)
    return {
        "gradients": normal_values(seeds[0], (N_DP, D, F), 1.0, 6.0, ((0, 2), (1, 4), (2, 16))),
        "left_basis": normal_values(seeds[1], (D, D), D ** -0.5, 0.125, ((0, 16), (1, 4))),
        "right_basis": normal_values(seeds[2], (F, F), F ** -0.5, 0.046875, ((0, 16), (1, 8))),
        "first_moment": normal_values(seeds[3], (D, F), 0.3, 1.8, ((0, 16), (1, 8)), jnp.float32),
        "second_moment": jnp.clip(jnp.exp(math.log(0.5) - 3.218876 * jax.random.uniform(seeds[4], (D, F), jnp.float32) ** levels(seeds[4], (D, F), ((0, 16), (1, 8)), -0.2, 0.2)), 0.02, 0.5),
        "omega_left": normal_values(seeds[5], (D, K), D ** -0.5, 0.125),
        "omega_right": normal_values(seeds[6], (F, K), F ** -0.5, 0.046875, ((0, 16),)),
        "sketch_left": normal_values(seeds[7], (D, K), 1.0, 6.0, ((0, 128),), jnp.float32),
        "sketch_right": normal_values(seeds[8], (F, K), 1.0, 6.0, ((0, 16),), jnp.float32),
    }


def rounded(values):
    return lax.optimization_barrier(values.astype(jnp.bfloat16)).astype(jnp.float32)

def reference(gradients, left_basis, right_basis, first_moment, second_moment, omega_left, omega_right, sketch_left, sketch_right):
    contract_rows = (((0,), (0,)), ((), ()))
    contract_cols = (((1,), (1,)), ((), ()))
    total = jnp.zeros((D, F), jnp.float32)
    for replica in range(N_DP):
        total = total + lax.dot_general(left_basis, gradients[replica], contract_rows, preferred_element_type=jnp.float32)
    rotated_left = (total / N_DP).astype(jnp.bfloat16)
    col_width = F // N_COL
    rotated = jnp.zeros((D, F), jnp.float32)
    for block in range(N_COL):
        lower = block * col_width
        rotated = rotated + rounded(jnp.dot(rotated_left[:, lower:lower + col_width], right_basis[lower:lower + col_width, :], preferred_element_type=jnp.float32))
    first_new = 0.9 * first_moment + 0.1 * rotated
    second_new = 0.95 * second_moment + 0.05 * rotated * rotated
    direction = (first_new / (jnp.sqrt(second_new) + 1e-08)).astype(jnp.bfloat16)
    groups = N_ROW * N_DP
    slab = F // groups
    back = jnp.zeros((D, F), jnp.float32)
    for block in range(groups):
        lower = block * slab
        back = back + rounded(lax.dot_general(direction[:, lower:lower + slab], right_basis[:, lower:lower + slab], contract_cols, preferred_element_type=jnp.float32))
    back_rotated = back.astype(jnp.bfloat16)
    band = D // groups
    summed = jnp.zeros((D, F), jnp.float32)
    for block in range(groups):
        lower = block * band
        summed = summed + rounded(jnp.dot(left_basis[:, lower:lower + band], back_rotated[lower:lower + band, :], preferred_element_type=jnp.float32))
    update = summed.astype(jnp.bfloat16)
    left_sum = jnp.zeros((D, K), jnp.float32)
    right_sum = jnp.zeros((F, K), jnp.float32)
    for replica in range(N_DP):
        gradient = gradients[replica]
        probe_left = lax.dot_general(gradient, omega_left, contract_rows, preferred_element_type=jnp.float32).astype(jnp.bfloat16)
        left_sum = left_sum + jnp.dot(gradient, probe_left, preferred_element_type=jnp.float32)
        probe_right = jnp.dot(gradient, omega_right, preferred_element_type=jnp.float32).astype(jnp.bfloat16)
        right_sum = right_sum + lax.dot_general(gradient, probe_right, contract_rows, preferred_element_type=jnp.float32)
    left_new = 0.5 * sketch_left + 0.5 * left_sum / (N_DP * math.sqrt(F))
    right_new = 0.5 * sketch_right + 0.5 * right_sum / (N_DP * math.sqrt(D))
    return (update, first_new, second_new, left_new, right_new)
```

```python
import math

import jax
import jax.numpy as jnp
from jax import lax
from jax.sharding import PartitionSpec as P

CHUNKS = 2
BF16 = jnp.bfloat16
F32 = jnp.float32


def dot(a, b, dims=((1,), (0,))):
    return lax.dot_general(a, b, (dims, ((), ())), preferred_element_type=F32)


def move(x, axis, target):
    n = lax.axis_size(axis)
    return lax.ppermute(x, axis, [(i, target(i) % n) for i in range(n)])


def on_device(
    gradients,
    left_basis,
    right_basis,
    first_moment,
    second_moment,
    omega_left,
    omega_right,
    sketch_left,
    sketch_right,
):
    n_row, n_col, n_dp = lax.axis_size("row"), lax.axis_size("col"), lax.axis_size("dp")
    row, col, dp = lax.axis_index("row"), lax.axis_index("col"), lax.axis_index("dp")
    y, z_lo, core = col // 4, (col // 2) % 2, col % 2
    n_y = n_col // 4
    own_grad = gradients[0]
    slab, width = own_grad.shape
    rows = slab * n_row
    k_dim = omega_left.shape[1]
    share = rows // n_col
    step = share // CHUNKS
    span = right_basis.shape[1]

    def swap_dp(x):
        return move(x, "dp", lambda i: i ^ 1)

    def swap_core(x):
        return move(x, "col", lambda i: i ^ 1)

    def swap_z(x):
        return move(x, "col", lambda i: i ^ 2)

    def to_row(x, s):
        return move(x, "row", lambda i: i + s)

    def to_y(x, s):
        return move(x, "col", lambda i: i + 4 * s)

    basis_wide = lax.all_gather(left_basis, "row", axis=1, tiled=True)
    by_chunk = basis_wide.reshape(share, n_col, CHUNKS, step).transpose(2, 0, 1, 3)
    basis = [
        lax.all_gather(by_chunk[k].reshape(share, n_col * step), "col", axis=0, tiled=True)
        for k in range(CHUNKS)
    ]

    omega_rows = lax.dynamic_slice_in_dim(omega_left, row * slab, slab, 0)
    probe_part = dot(omega_rows, own_grad, ((0,), (0,))).astype(BF16)
    half = slab // 2
    total = jnp.zeros((rows, width), BF16)
    probe_left_t = probe_part.astype(F32)
    for h in range(2):
        mine = own_grad[h * half : (h + 1) * half]
        summed = (mine.astype(F32) + swap_dp(mine).astype(F32)).astype(BF16)
        sent = summed if h == 0 else jnp.concatenate([summed, probe_part], 0)
        total = lax.dynamic_update_slice_in_dim(total, summed, row * slab + h * half, 0)
        for s in (1, 3, 2):
            got = to_row(sent, s)
            source = (row + n_row - s) % n_row
            total = lax.dynamic_update_slice_in_dim(
                total, got[:half], source * slab + h * half, 0
            )
            if h == 1:
                probe_left_t = probe_left_t + got[half:].astype(F32)
    probe_left_t = probe_left_t.astype(BF16)
    left_terms = dot(own_grad, probe_left_t, ((1,), (1,)))
    right_terms = dot(own_grad, omega_right)
    part = slab // n_col
    sketch_terms = jnp.concatenate(
        [right_terms.reshape(n_col, part, k_dim), left_terms.reshape(n_col, part, k_dim)], 1
    )

    def halves(x, index):
        x = x.reshape(n_col // 2, 2, x.shape[0] // n_col, x.shape[1])
        return lax.dynamic_index_in_dim(x, index, 1, keepdims=False)

    first_parts, second_parts, backs = [], [], []
    for k in range(CHUNKS):
        rotated_left = (0.5 * dot(basis[k], total, ((0,), (0,)))).astype(BF16)

        def products(index):
            block = halves(rotated_left, index)
            out = dot(block.reshape(-1, width), right_basis).reshape(n_col // 2, step, span)
            if k == 0:
                extra = lax.dynamic_index_in_dim(
                    sketch_terms.reshape(n_col // 2, 2, 2 * part, k_dim), index, 1, keepdims=False
                )
                extra = extra.reshape(n_col // 2, step, -1)
                out = jnp.concatenate([out, extra], 2)
            return out

        theirs = swap_core(products(1 - core).astype(BF16))
        pair = (products(core) + theirs.astype(F32)).astype(BF16)
        pair = pair.reshape(n_y, 2, step, -1)
        column = lax.dynamic_index_in_dim(pair, y, 0, keepdims=False).astype(F32)
        for s in (1, 3, 2):
            sent = lax.dynamic_index_in_dim(pair, (y + s) % n_y, 0, keepdims=False)
            column = column + to_y(sent, s).astype(F32)
        sent = lax.dynamic_index_in_dim(column, 1 - z_lo, 0, keepdims=False).astype(BF16)
        own = lax.dynamic_index_in_dim(column, z_lo, 0, keepdims=False)
        own = own + swap_z(sent).astype(F32)
        rotated = own[:, :span]
        lower = k * step
        first_new = 0.9 * first_moment[lower : lower + step] + 0.1 * rotated
        second_new = 0.95 * second_moment[lower : lower + step] + 0.05 * rotated * rotated
        direction = (first_new / (jnp.sqrt(second_new) + 1e-08)).astype(BF16)
        first_parts.append(first_new)
        second_parts.append(second_new)
        if k == 0:
            sketch_sum = own[:, span:].reshape(2 * part, k_dim)
        gathered = lax.all_gather(direction, "col", axis=0, tiled=True)
        backs.append(dot(gathered, right_basis, ((1,), (1,))).astype(BF16))
        if k == 0:
            probe_sum = lax.all_gather(
                sketch_sum[:part].astype(BF16), "col", axis=0, tiled=True
            )

    lines = part // n_dp
    left_mine = lax.dynamic_slice_in_dim(sketch_sum, part + dp * lines, lines, 0)
    left_sent = lax.dynamic_slice_in_dim(sketch_sum, part + (1 - dp) * lines, lines, 0)
    left_sum = left_mine + swap_dp(left_sent.astype(BF16)).astype(F32)
    f_dim = width * n_col
    left_new = 0.5 * sketch_left + 0.5 * left_sum / (n_dp * math.sqrt(f_dim))

    right_part = dot(own_grad, probe_sum, ((0,), (0,)))
    right_sent = right_part.astype(BF16)
    for s in (1, 3, 2):
        right_part = right_part + to_row(right_sent, s).astype(F32)
    right_sum = right_part.astype(BF16).astype(F32) + swap_dp(right_part.astype(BF16)).astype(F32)
    right_new = 0.5 * sketch_right + 0.5 * right_sum / (n_dp * math.sqrt(rows))

    def update_part(index):
        out = 0.0
        for k in range(CHUNKS):
            block = lax.dynamic_slice_in_dim(basis[k], index * slab, slab, 0)
            out = out + dot(block, backs[k])
        return out.astype(BF16).reshape(n_dp, 2, slab // 4, width)

    parts = {s: update_part((row + s) % n_row) for s in (1, 3, 2, 0)}
    update = []
    for h in range(2):
        acc = parts[0][:, h].astype(F32)
        for s in (1, 3, 2):
            acc = acc + to_row(parts[s][:, h], s).astype(F32)
        sent = lax.dynamic_index_in_dim(acc, 1 - dp, 0, keepdims=False).astype(BF16)
        own = lax.dynamic_index_in_dim(acc, dp, 0, keepdims=False)
        update.append((own + swap_dp(sent).astype(F32)).astype(BF16))
    return (
        jnp.concatenate(update, 0),
        jnp.concatenate(first_parts, 0),
        jnp.concatenate(second_parts, 0),
        left_new,
        right_new,
    )


def solution(mesh):
    return jax.shard_map(
        on_device,
        mesh=mesh,
        in_specs=(
            P("dp", "row", "col"),
            P("col", "row"),
            P("col", ("row", "dp")),
            P("col", ("row", "dp")),
            P("col", ("row", "dp")),
            P(),
            P("col", None),
            P(("row", "col", "dp"), None),
            P("col", None),
        ),
        out_specs=(
            P(("row", "dp"), "col"),
            P("col", ("row", "dp")),
            P("col", ("row", "dp")),
            P(("row", "col", "dp"), None),
            P("col", None),
        ),
        check_vma=False,
    )
```

```python
import math

import jax
import jax.numpy as jnp
from jax import lax
from jax.experimental import pallas as pl
from jax.experimental.pallas import tpu as pltpu
from jax.sharding import PartitionSpec as P

BF16 = jnp.bfloat16
F32 = jnp.float32


def dot(a, b, dims=((1,), (0,))):
    return lax.dot_general(a, b, (dims, ((), ())), preferred_element_type=F32)


def move(x, axis, target):
    n = lax.axis_size(axis)
    return lax.ppermute(x, axis, [(i, target(i) % n) for i in range(n)])


def swap_dp(x):
    return move(x, "dp", lambda i: i ^ 1)


def swap_core(x):
    return move(x, "col", lambda i: i ^ 1)


def swap_z(x):
    return move(x, "col", lambda i: i ^ 2)


def to_row(x, s):
    return move(x, "row", lambda i: i + s)


def to_y(x, s):
    return move(x, "col", lambda i: i + 4 * s)


def params():
    return pltpu.CompilerParams(vmem_limit_bytes=40 * 2**20)


CHEAP = pl.CostEstimate(flops=1000, bytes_accessed=1000, transcendentals=0)
ANY = pl.BlockSpec(memory_space=pl.ANY)


def whole(x):
    return pl.BlockSpec(x.shape, lambda t, *c: (0,) * x.ndim)


def sum_pair(a, b, scale, after, name):
    def body(a_ref, b_ref, *refs):
        refs[-1][...] = (scale * (a_ref[...].astype(F32) + b_ref[...].astype(F32))).astype(BF16)

    return pl.pallas_call(
        body,
        grid=(1,),
        in_specs=[whole(a), whole(b)] + [ANY] * len(after),
        out_specs=whole(a),
        out_shape=jax.ShapeDtypeStruct(a.shape, BF16),
        compiler_params=params(),
        cost_estimate=CHEAP,
        name=name,
    )(a, b, *after)


def sum_blocks(index, blocks, after, name):
    n = len(blocks)
    rows, columns = blocks[0].shape
    size = rows // 2

    def body(index_ref, *refs):
        keep, send = refs[-2:]
        for out, lower in ((keep, index_ref[0] * size), (send, (1 - index_ref[0]) * size)):
            lower = pl.multiple_of(lower, 16)
            acc = refs[0][pl.ds(lower, size), :].astype(F32)
            for ref in refs[1:n]:
                acc = acc + ref[pl.ds(lower, size), :].astype(F32)
            out[...] = acc.astype(out.dtype)

    return pl.pallas_call(
        body,
        grid_spec=pltpu.PrefetchScalarGridSpec(
            num_scalar_prefetch=1,
            grid=(1,),
            in_specs=[whole(b) for b in blocks] + [ANY] * len(after),
            out_specs=[pl.BlockSpec((size, columns), lambda t, c: (0, 0))] * 2,
        ),
        out_shape=[
            jax.ShapeDtypeStruct((size, columns), F32),
            jax.ShapeDtypeStruct((size, columns), BF16),
        ],
        compiler_params=params(),
        cost_estimate=CHEAP,
        name=name,
    )(index.reshape(1), *blocks, *after)


def place(pieces, starts, shape, after, name):
    dtype = pieces[0][0].dtype
    arrays = []
    for piece in pieces:
        if not any(piece[0] is x for x in arrays):
            arrays.append(piece[0])
    where = [[x is piece[0] for x in arrays].index(True) for piece in pieces]

    def body(starts_ref, *refs):
        out = refs[-1]
        for i, (_, lower, count, source, target) in enumerate(pieces):
            start = pl.multiple_of(starts_ref[i], 16)
            out[pl.ds(start, count), target] = refs[where[i]][lower : lower + count, source]

    once = pl.Buffered(1)
    return pl.pallas_call(
        body,
        grid_spec=pltpu.PrefetchScalarGridSpec(
            num_scalar_prefetch=1,
            grid=(1,),
            in_specs=[
                pl.BlockSpec(x.shape, lambda t, c: (0, 0), pipeline_mode=once) for x in arrays
            ]
            + [ANY] * len(after),
            out_specs=pl.BlockSpec(shape, lambda t, c: (0, 0), pipeline_mode=once),
        ),
        out_shape=jax.ShapeDtypeStruct(shape, dtype),
        compiler_params=params(),
        cost_estimate=CHEAP,
        name=name,
    )(jnp.stack(starts).astype(jnp.int32), *arrays, *after)


def probe(grad, omega, after, name):
    size = (grad.shape[1], omega.shape[1])

    def body(g_ref, o_ref, *refs):
        refs[-1][...] = dot(g_ref[...], o_ref[...], ((0,), (0,))).astype(BF16)

    return pl.pallas_call(
        body,
        grid=(1,),
        in_specs=[whole(grad), whole(omega)] + [ANY] * len(after),
        out_specs=pl.BlockSpec(size, lambda t: (0, 0)),
        out_shape=jax.ShapeDtypeStruct(size, BF16),
        compiler_params=params(),
        cost_estimate=CHEAP,
        name=name,
    )(grad, omega, *after)


def rotate(index, basis, total, right, extra, after, name):
    rows, width = total.shape
    size = basis.shape[1] // 2
    span = right.shape[1] // 2
    wide = span + extra.shape[1]
    tiles = 2
    tile = size // tiles
    once = pl.Buffered(1)

    def body(index_ref, basis_ref, total_ref, right_ref, extra_ref, *refs):
        left_out, out = refs[-2:]
        left = (0.5 * dot(basis_ref[...], total_ref[...], ((0,), (0,)))).astype(BF16)
        left_out[...] = left
        out[:, :span] = dot(left, right_ref[...]).astype(BF16)
        out[:, span:] = extra_ref[...]

    return pl.pallas_call(
        body,
        grid_spec=pltpu.PrefetchScalarGridSpec(
            num_scalar_prefetch=1,
            grid=(tiles,),
            in_specs=[
                pl.BlockSpec((rows, tile), lambda t, c: (0, c[0] * tiles + t)),
                pl.BlockSpec((rows, width), lambda t, c: (0, 0), pipeline_mode=once),
                pl.BlockSpec((width, span), lambda t, c: (0, 1), pipeline_mode=once),
                pl.BlockSpec((tile, extra.shape[1]), lambda t, c: (c[0] * tiles + t, 0)),
            ]
            + [ANY] * len(after),
            out_specs=[
                pl.BlockSpec((tile, width), lambda t, c: (t, 0)),
                pl.BlockSpec((tile, wide), lambda t, c: (t, 0)),
            ],
        ),
        out_shape=[
            jax.ShapeDtypeStruct((size, width), BF16),
            jax.ShapeDtypeStruct((size, wide), BF16),
        ],
        compiler_params=params(),
        cost_estimate=CHEAP,
        name=name,
    )(index.reshape(1), basis, total, right, extra, *after)


def rotate_rest(left, right, after, name):
    rows, width = left.shape
    span = right.shape[1] // 2
    tile = rows // 2

    def body(left_ref, right_ref, *refs):
        refs[-1][...] = dot(left_ref[...], right_ref[...]).astype(BF16)

    return pl.pallas_call(
        body,
        grid=(2,),
        in_specs=[
            pl.BlockSpec((tile, width), lambda t: (t, 0)),
            pl.BlockSpec((width, span), lambda t: (0, 0), pipeline_mode=pl.Buffered(1)),
        ]
        + [ANY] * len(after),
        out_specs=pl.BlockSpec((tile, span), lambda t: (t, 0)),
        out_shape=jax.ShapeDtypeStruct((rows, span), BF16),
        compiler_params=params(),
        cost_estimate=CHEAP,
        name=name,
    )(left, right, *after)


def split_parts(index, mine, theirs, n_y, name):
    rows, columns = mine.shape
    size = rows // n_y // 2

    def body(index_ref, a_ref, b_ref, keep, send):
        for out, lower in ((keep, index_ref[0] * size), (send, (1 - index_ref[0]) * size)):
            at = pl.ds(pl.multiple_of(lower, 16), size)
            out[...] = (a_ref[at, :].astype(F32) + b_ref[at, :].astype(F32)).astype(BF16)

    return pl.pallas_call(
        body,
        grid_spec=pltpu.PrefetchScalarGridSpec(
            num_scalar_prefetch=1,
            grid=(n_y,),
            in_specs=[pl.BlockSpec((2 * size, columns), lambda t, c: (t, 0))] * 2,
            out_specs=[pl.BlockSpec((size, columns), lambda t, c: (t, 0))] * 2,
        ),
        out_shape=[jax.ShapeDtypeStruct((rows // 2, columns), BF16)] * 2,
        compiler_params=params(),
        cost_estimate=CHEAP,
        name=name,
    )(index.reshape(1), mine, theirs)


def add_parts(first, mine, theirs, n_y, name):
    rows, columns = mine.shape
    size = rows // n_y

    def body(first_ref, a_ref, b_ref, *outs):
        value = (a_ref[...].astype(F32) + b_ref[...].astype(F32)).astype(BF16)
        for i in range(n_y):

            @pl.when(pl.program_id(0) == i)
            def _():
                outs[i][...] = value

    block = pl.BlockSpec((size, columns), lambda s, c: ((c[0] + n_y - s) % n_y, 0))
    return pl.pallas_call(
        body,
        grid_spec=pltpu.PrefetchScalarGridSpec(
            num_scalar_prefetch=1,
            grid=(n_y,),
            in_specs=[block, block],
            out_specs=[pl.BlockSpec((size, columns), lambda s, c: (0, 0))] * n_y,
        ),
        out_shape=[jax.ShapeDtypeStruct((size, columns), BF16)] * n_y,
        compiler_params=params(),
        cost_estimate=CHEAP,
        name=name,
    )(first.reshape(1), mine, theirs)


def rotate_back(parts, right, after, name):
    rows, width = parts[0].shape[0], right.shape[0]
    n = len(parts)
    size = right.shape[1] // n
    tile = rows // 2

    def body(r_ref, *refs):
        acc = 0.0
        for i in range(n):
            acc = acc + dot(refs[i][...], r_ref[:, i * size : (i + 1) * size], ((1,), (1,)))
        refs[-1][...] = acc.astype(BF16)

    return pl.pallas_call(
        body,
        grid=(2,),
        in_specs=[
            pl.BlockSpec(right.shape, lambda t: (0, 0), pipeline_mode=pl.Buffered(1)),
        ]
        + [pl.BlockSpec((tile, size), lambda t: (t, 0))] * n
        + [ANY] * len(after),
        out_specs=pl.BlockSpec((tile, width), lambda t: (t, 0)),
        out_shape=jax.ShapeDtypeStruct((rows, width), BF16),
        compiler_params=params(),
        cost_estimate=CHEAP,
        name=name,
    )(right, *parts, *after)


def update_rows(ids, basis, backs, slab, cuts, lower, upper, after, name):
    n = ids.shape[0] - 1
    tile = slab // cuts
    columns = upper - lower
    depth, width = backs[0].shape
    once = pl.Buffered(1)

    def body(ids_ref, a_ref, b_ref, back_a, back_b, *refs):
        acc = dot(a_ref[...], back_a[:, lower:upper]) + dot(b_ref[...], back_b[:, lower:upper])
        refs[-1][...] = acc.astype(BF16)

    return pl.pallas_call(
        body,
        grid_spec=pltpu.PrefetchScalarGridSpec(
            num_scalar_prefetch=1,
            grid=(cuts * n,),
            in_specs=[
                pl.BlockSpec((tile, depth), lambda t, c: (c[1 + t // cuts] * cuts + t % cuts, c[0])),
                pl.BlockSpec((tile, depth), lambda t, c: (c[1 + t // cuts] * cuts + t % cuts, 1 - c[0])),
                pl.BlockSpec((depth, width), lambda t, c: (0, 0), pipeline_mode=once),
                pl.BlockSpec((depth, width), lambda t, c: (0, 0), pipeline_mode=once),
            ]
            + [ANY] * len(after),
            out_specs=pl.BlockSpec((tile, columns), lambda t, c: (t, 0)),
        ),
        out_shape=jax.ShapeDtypeStruct((n * slab, columns), BF16),
        compiler_params=params(),
        cost_estimate=CHEAP,
        name=name,
    )(ids.astype(jnp.int32), basis, basis, *backs, *after)


def on_device(
    gradients,
    left_basis,
    right_basis,
    first_moment,
    second_moment,
    omega_left,
    omega_right,
    sketch_left,
    sketch_right,
):
    n_row, n_col, n_dp = lax.axis_size("row"), lax.axis_size("col"), lax.axis_size("dp")
    row, col, dp = lax.axis_index("row"), lax.axis_index("col"), lax.axis_index("dp")
    y, z_lo, core = col // 4, (col // 2) % 2, col % 2
    n_y = n_col // 4
    own_grad = gradients[0]
    slab, width = own_grad.shape
    rows = slab * n_row
    k_dim = omega_left.shape[1]
    share = rows // n_col
    span = right_basis.shape[1]
    part = slab // n_col
    half = slab // 2

    every = (slice(None), slice(None))
    source_rows = [(row + n_row - s) % n_row for s in (0, 1, 3, 2)]

    other_top = swap_dp(own_grad[:half])
    came = {0: left_basis}
    for s in (1, 3, 2):
        came[s] = to_row(left_basis, s)

    omega_rows = lax.dynamic_slice_in_dim(omega_left, row * slab, slab, 0)
    probe_sent = probe(own_grad, omega_rows, (other_top, came[1], came[2], came[3]), "probe_left")
    probe_came = [to_row(probe_sent, s) for s in (1, 3, 2)]
    kept, sent = sum_blocks(jnp.int32(0), [probe_sent] + probe_came, (), "probe_sum")
    probe_left = jnp.concatenate([kept.astype(BF16), sent], 0)

    other_grad = jnp.concatenate([other_top, swap_dp(own_grad[half:])], 0)
    summed = sum_pair(own_grad, other_grad, 1.0, (kept,), "sum_replicas")
    blocks = [summed] + [to_row(summed, s) for s in (1, 3, 2)]

    pieces = []
    for c in range(2):
        for s in range(n_row):
            for z in range(2):
                source, target = (2 * z + c) * share, ((c * n_row + s) * 2 + z) * share
                pieces.append(
                    (came[s], 0, share, slice(source, source + share), slice(target, target + share))
                )
    wide = place(pieces, [jnp.int32(0)] * len(pieces), (share, rows), (other_top,), "left_basis_rows")
    basis = lax.all_gather(wide, "col", axis=0, tiled=True)

    def by_y(x, axis):
        return jnp.roll(jnp.flip(x, axis), row - (n_y - 1), axis)

    def by_owner(terms):
        terms = terms.astype(BF16).reshape(n_y, 2, 2, part, k_dim).transpose(2, 0, 1, 3, 4)
        return by_y(terms, 1).reshape(n_col, part, k_dim)

    right_terms = dot(own_grad, omega_right)
    left_terms = dot(own_grad, probe_left)
    extra = jnp.concatenate([by_owner(right_terms), by_owner(left_terms)], 1)
    extra = jnp.pad(extra, ((0, 0), (0, share - 2 * part), (0, 0))).reshape(-1, k_dim)
    total = place(
        [(x, 0, slab, *every) for x in blocks],
        [i * slab for i in source_rows],
        (rows, width),
        (extra,),
        "summed_gradient",
    )

    first = (row - y + n_y) % n_y
    left_theirs, sent_b = rotate(
        1 - core, basis, total, right_basis, extra, (), "rotate_theirs_b"
    )
    other_b = swap_core(sent_b)
    left_mine, mine_b = rotate(
        core, basis, total, right_basis, extra, (sent_b,), "rotate_mine_b"
    )
    keep_b, sent_b = split_parts(z_lo, mine_b, other_b, n_y, "pair_b")
    came_b = swap_z(sent_b)
    sent_a = rotate_rest(left_theirs, right_basis, (keep_b,), "rotate_theirs_a")
    other_a = swap_core(sent_a)
    mine_a = rotate_rest(left_mine, right_basis, (sent_a,), "rotate_mine_a")
    parts_a = add_parts(first, mine_a, other_a, n_y, "pair_a")
    came_a = [to_y(parts_a[s], s) for s in (1, 3, 2)]
    parts_b = add_parts(first, keep_b, came_b, n_y, "column_b")
    own_a, sent_a = sum_blocks(z_lo, [parts_a[0]] + came_a, (parts_b[0],), "column_a")
    came_a = swap_z(sent_a)
    own_b = parts_b[0].astype(F32)
    for s in (1, 3, 2):
        own_b = own_b + to_y(parts_b[s], s).astype(F32)
    own_a = own_a + came_a.astype(F32)

    middle = span // 2
    firsts, seconds, directions = [], [], []
    for lower, rotated in ((0, own_a), (middle, own_b[:, :middle])):
        at = slice(lower, lower + middle)
        first_part = 0.9 * first_moment[:, at] + 0.1 * rotated
        second_part = 0.95 * second_moment[:, at] + 0.05 * rotated * rotated
        directions.append((first_part / (jnp.sqrt(second_part) + 1e-08)).astype(BF16))
        firsts.append(first_part)
        seconds.append(second_part)
    first_new = jnp.concatenate(firsts, 1)
    second_new = jnp.concatenate(seconds, 1)
    sketches = own_b[:, middle:]

    mine_b = jnp.concatenate([directions[1], sketches.astype(BF16)], 1)
    came_b = [mine_b] + [to_y(mine_b, s) for s in (1, 3, 2)]
    other = swap_z(directions[0])
    mine_a = jnp.where(
        z_lo == 0,
        jnp.concatenate([directions[0], other], 0),
        jnp.concatenate([other, directions[0]], 0),
    )
    came_a = [mine_a] + [to_y(mine_a, s) for s in (1, 3, 2)]
    order = [(first + s) % n_y for s in (0, 1, 3, 2)]
    near_b = place(
        [(x, 0, share, *every) for x in came_b],
        [i * share for i in order],
        (n_y * share, mine_b.shape[1]),
        (mine_a,),
        "direction_near_b",
    )
    far_b = swap_z(near_b)
    own_a = place(
        [(x, 0, 2 * share, *every) for x in came_a],
        [i * 2 * share for i in order],
        (2 * n_y * share, middle),
        (),
        "direction_a",
    )
    pieces = [(x, s * share, share, *every) for x in (near_b, far_b) for s in range(n_y)]
    starts = [2 * s * share + z * share for z in (z_lo, 1 - z_lo) for s in range(n_y)]
    own_b = place(pieces, starts, (2 * n_y * share, mine_b.shape[1]), (own_a,), "direction_b")
    other_a, other_b = swap_core(own_a), swap_core(own_b)
    back_own = rotate_back([own_a, own_b], right_basis, (), "back_own")
    back_other = rotate_back([other_a, other_b], right_basis, (back_own,), "back_other")

    probes = [
        by_y(p[:, middle:].reshape(n_y, 2, share, k_dim)[:, :, :part], 0) for p in (own_b, other_b)
    ]
    probes = jnp.where(core == 0, jnp.stack(probes, 2), jnp.stack(probes[::-1], 2))
    right_part = probe(own_grad, probes.reshape(slab, k_dim), (back_other,), "right_terms")
    right_came = [to_row(right_part, s) for s in (1, 3, 2)]

    lines = part // n_dp
    left_mine = lax.dynamic_slice_in_dim(sketches, part + dp * lines, lines, 0)
    left_sent = lax.dynamic_slice_in_dim(sketches, part + (1 - dp) * lines, lines, 0)
    left_sum = left_mine + swap_dp(left_sent.astype(BF16)).astype(F32)
    f_dim = width * n_col
    left_new = 0.5 * sketch_left + 0.5 * left_sum / (n_dp * math.sqrt(f_dim))

    late = width * 2 // 7
    early = width - late
    backs = [back_own, back_other]
    slabs = [(row + s) % n_row for s in range(n_row)]
    far = update_rows(
        jnp.stack([core] + slabs[1:]), basis, backs, slab, 2, 0, early, (right_part,), "update_far"
    )
    came = [to_row(far[(s - 1) * slab : s * slab], s) for s in (2, 1, 3)]
    all_late = update_rows(
        jnp.stack([core] + slabs), basis, backs, slab, 1, early, width, (far,), "update_late"
    )
    kept, sent = sum_blocks(dp, [right_part] + right_came, (all_late,), "right_sum")
    kept = kept.astype(BF16)
    right_mine = jnp.where(
        dp == 0, jnp.concatenate([kept, sent], 0), jnp.concatenate([sent, kept], 0)
    )
    all_late = all_late.reshape(n_row, n_dp, half, late)
    sent = lax.dynamic_index_in_dim(all_late, 1 - dp, 1, keepdims=False).reshape(-1, late)
    kept = lax.dynamic_index_in_dim(all_late, dp, 1, keepdims=False).reshape(-1, late)
    other = swap_dp(sent)
    near = update_rows(
        jnp.stack([core] + slabs[:1]), basis, backs, slab, 2, 0, early, (sent,), "update_near"
    )
    pair = sum_pair(kept, other, 1.0, (near,), "update_pair")
    late_came = [to_row(pair[s * half : (s + 1) * half], s) for s in (2, 1, 3)]
    own, sent = sum_blocks(dp, [near] + came, (pair,), "update_early")
    update_early = (own + swap_dp(sent).astype(F32)).astype(BF16)
    acc = pair[:half].astype(F32)
    for block in late_came:
        acc = acc + block.astype(F32)
    update = jnp.concatenate([update_early, acc.astype(BF16)], 1)

    right_sum = right_mine.astype(F32) + swap_dp(right_mine).astype(F32)
    right_new = 0.5 * sketch_right + 0.5 * right_sum / (n_dp * math.sqrt(rows))
    return (
        update,
        first_new,
        second_new,
        left_new,
        right_new,
    )


def solution(mesh):
    return jax.shard_map(
        on_device,
        mesh=mesh,
        in_specs=(
            P("dp", "row", "col"),
            P("col", "row"),
            P("col", ("row", "dp")),
            P("col", ("row", "dp")),
            P("col", ("row", "dp")),
            P(),
            P("col", None),
            P(("row", "col", "dp"), None),
            P("col", None),
        ),
        out_specs=(
            P(("row", "dp"), "col"),
            P("col", ("row", "dp")),
            P("col", ("row", "dp")),
            P(("row", "col", "dp"), None),
            P("col", None),
        ),
        check_vma=False,
    )
```

```python
import math

import jax
import jax.numpy as jnp
from jax import lax
from jax.experimental import pallas as pl
from jax.experimental.pallas import tpu as pltpu
from jax.sharding import PartitionSpec as P

BF16 = jnp.bfloat16
F32 = jnp.float32


def dot(a, b, dims=((1,), (0,))):
    return lax.dot_general(a, b, (dims, ((), ())), preferred_element_type=F32)


def move(x, axis, target):
    n = lax.axis_size(axis)
    return lax.ppermute(x, axis, [(i, target(i) % n) for i in range(n)])


def swap_dp(x):
    return move(x, "dp", lambda i: i ^ 1)


def swap_core(x):
    return move(x, "col", lambda i: i ^ 1)


def swap_z(x):
    return move(x, "col", lambda i: i ^ 2)


def to_row(x, s):
    return move(x, "row", lambda i: i + s)


def to_y(x, s):
    return move(x, "col", lambda i: i + 4 * s)


def params():
    return pltpu.CompilerParams(vmem_limit_bytes=40 * 2**20)


BLOCK = 256
BLOCKS_B = 3
CHEAP = pl.CostEstimate(flops=1000, bytes_accessed=1000, transcendentals=0)
HEAVY = pl.CostEstimate(flops=10**11, bytes_accessed=10**8, transcendentals=0)
ANY = pl.BlockSpec(memory_space=pl.ANY)


def whole(x):
    return pl.BlockSpec(x.shape, lambda t, *c: (0,) * x.ndim)


def sum_replicas(grad, others, omega, name):
    rows, columns = grad.shape
    k_dim = omega.shape[1]

    def body(grad_ref, omega_ref, *refs):
        out = refs[-1]
        lower = 0
        for ref in refs[:-1]:
            at = slice(lower, lower + ref.shape[0])
            out[at, :] = (grad_ref[at, :].astype(F32) + ref[...].astype(F32)).astype(BF16)
            lower += ref.shape[0]
        out[rows:, :] = dot(omega_ref[...], grad_ref[...], ((0,), (0,))).astype(BF16)

    return pl.pallas_call(
        body,
        grid=(1,),
        in_specs=[whole(grad), whole(omega)] + [whole(x) for x in others],
        out_specs=pl.BlockSpec((rows + k_dim, columns), lambda t: (0, 0)),
        out_shape=jax.ShapeDtypeStruct((rows + k_dim, columns), BF16),
        compiler_params=params(),
        cost_estimate=CHEAP,
        name=name,
    )(grad, omega, *others)


def sum_pair(a, b, scale, after, name):
    def body(a_ref, b_ref, *refs):
        refs[-1][...] = (scale * (a_ref[...].astype(F32) + b_ref[...].astype(F32))).astype(BF16)

    return pl.pallas_call(
        body,
        grid=(1,),
        in_specs=[whole(a), whole(b)] + [ANY] * len(after),
        out_specs=whole(a),
        out_shape=jax.ShapeDtypeStruct(a.shape, BF16),
        compiler_params=params(),
        cost_estimate=CHEAP,
        name=name,
    )(a, b, *after)


def sum_blocks(index, blocks, after, name):
    n = len(blocks)
    rows, columns = blocks[0].shape
    size = rows // 2

    def body(index_ref, *refs):
        keep, send = refs[-2:]
        for out, lower in ((keep, index_ref[0] * size), (send, (1 - index_ref[0]) * size)):
            lower = pl.multiple_of(lower, 16)
            acc = refs[0][pl.ds(lower, size), :].astype(F32)
            for ref in refs[1:n]:
                acc = acc + ref[pl.ds(lower, size), :].astype(F32)
            out[...] = acc.astype(out.dtype)

    return pl.pallas_call(
        body,
        grid_spec=pltpu.PrefetchScalarGridSpec(
            num_scalar_prefetch=1,
            grid=(1,),
            in_specs=[whole(b) for b in blocks] + [ANY] * len(after),
            out_specs=[pl.BlockSpec((size, columns), lambda t, c: (0, 0))] * 2,
        ),
        out_shape=[
            jax.ShapeDtypeStruct((size, columns), F32),
            jax.ShapeDtypeStruct((size, columns), BF16),
        ],
        compiler_params=params(),
        cost_estimate=CHEAP,
        name=name,
    )(index.reshape(1), *blocks, *after)


def place(pieces, starts, shape, after, name):
    dtype = pieces[0][0].dtype
    arrays = []
    for piece in pieces:
        if not any(piece[0] is x for x in arrays):
            arrays.append(piece[0])
    where = [[x is piece[0] for x in arrays].index(True) for piece in pieces]

    def body(starts_ref, *refs):
        out = refs[-1]
        for i, (_, lower, count, source, target) in enumerate(pieces):
            start = pl.multiple_of(starts_ref[i], 16)
            out[pl.ds(start, count), target] = refs[where[i]][lower : lower + count, source]

    once = pl.Buffered(1)
    return pl.pallas_call(
        body,
        grid_spec=pltpu.PrefetchScalarGridSpec(
            num_scalar_prefetch=1,
            grid=(1,),
            in_specs=[
                pl.BlockSpec(x.shape, lambda t, c: (0, 0), pipeline_mode=once) for x in arrays
            ]
            + [ANY] * len(after),
            out_specs=pl.BlockSpec(shape, lambda t, c: (0, 0), pipeline_mode=once),
        ),
        out_shape=jax.ShapeDtypeStruct(shape, dtype),
        compiler_params=params(),
        cost_estimate=CHEAP,
        name=name,
    )(jnp.stack(starts).astype(jnp.int32), *arrays, *after)


def probe(grad, omega, after, name):
    size = (grad.shape[1], omega.shape[1])

    def body(g_ref, o_ref, *refs):
        refs[-1][...] = dot(g_ref[...], o_ref[...], ((0,), (0,))).astype(BF16)

    return pl.pallas_call(
        body,
        grid=(1,),
        in_specs=[whole(grad), whole(omega)] + [ANY] * len(after),
        out_specs=pl.BlockSpec(size, lambda t: (0, 0)),
        out_shape=jax.ShapeDtypeStruct(size, BF16),
        compiler_params=params(),
        cost_estimate=CHEAP,
        name=name,
    )(grad, omega, *after)


def rotate(index, basis, total, right, extra, after, name):
    rows, width = total.shape
    size = basis.shape[1] // 2
    span = BLOCKS_B * BLOCK
    wide = span + extra.shape[1]
    tiles = 2
    tile = size // tiles
    once = pl.Buffered(1)

    def body(index_ref, basis_ref, total_ref, extra_ref, *refs):
        left_out, out = refs[-2:]
        left = (0.5 * dot(basis_ref[...], total_ref[...], ((0,), (0,)))).astype(BF16)
        left_out[...] = left
        for i in range(BLOCKS_B):
            at = slice(i * BLOCK, (i + 1) * BLOCK)
            out[:, at] = dot(left, refs[i][...]).astype(BF16)
        out[:, span:] = extra_ref[...]

    return pl.pallas_call(
        body,
        grid_spec=pltpu.PrefetchScalarGridSpec(
            num_scalar_prefetch=1,
            grid=(tiles,),
            in_specs=[
                pl.BlockSpec((rows, tile), lambda t, c: (0, c[0] * tiles + t)),
                pl.BlockSpec((rows, width), lambda t, c: (0, 0), pipeline_mode=once),
                pl.BlockSpec((tile, extra.shape[1]), lambda t, c: (c[0] * tiles + t, 0)),
            ]
            + [
                pl.BlockSpec((width, BLOCK), lambda t, c, i=i: (0, i), pipeline_mode=once)
                for i in range(BLOCKS_B)
            ]
            + [ANY] * len(after),
            out_specs=[
                pl.BlockSpec((tile, width), lambda t, c: (t, 0)),
                pl.BlockSpec((tile, wide), lambda t, c: (t, 0)),
            ],
        ),
        out_shape=[
            jax.ShapeDtypeStruct((size, width), BF16),
            jax.ShapeDtypeStruct((size, wide), BF16),
        ],
        compiler_params=params(),
        cost_estimate=CHEAP,
        name=name,
    )(index.reshape(1), basis, total, extra, *[right] * BLOCKS_B, *after)


def rotate_rest(left, right, after, name):
    rows, width = left.shape
    n = right.shape[1] // BLOCK - BLOCKS_B
    span = n * BLOCK
    tile = rows // 2

    def body(left_ref, *refs):
        for i in range(n):
            at = slice(i * BLOCK, (i + 1) * BLOCK)
            refs[-1][:, at] = dot(left_ref[...], refs[i][...]).astype(BF16)

    return pl.pallas_call(
        body,
        grid=(2,),
        in_specs=[
            pl.BlockSpec((tile, width), lambda t: (t, 0)),
        ]
        + [
            pl.BlockSpec(
                (width, BLOCK), lambda t, i=i: (0, BLOCKS_B + i), pipeline_mode=pl.Buffered(1)
            )
            for i in range(n)
        ]
        + [ANY] * len(after),
        out_specs=pl.BlockSpec((tile, span), lambda t: (t, 0)),
        out_shape=jax.ShapeDtypeStruct((rows, span), BF16),
        compiler_params=params(),
        cost_estimate=CHEAP,
        name=name,
    )(left, *[right] * n, *after)


def split_parts(index, mine, theirs, n_y, name):
    rows, columns = mine.shape
    size = rows // n_y // 2

    def body(index_ref, a_ref, b_ref, keep, send):
        for out, lower in ((keep, index_ref[0] * size), (send, (1 - index_ref[0]) * size)):
            at = pl.ds(pl.multiple_of(lower, 16), size)
            out[...] = (a_ref[at, :].astype(F32) + b_ref[at, :].astype(F32)).astype(BF16)

    return pl.pallas_call(
        body,
        grid_spec=pltpu.PrefetchScalarGridSpec(
            num_scalar_prefetch=1,
            grid=(n_y,),
            in_specs=[pl.BlockSpec((2 * size, columns), lambda t, c: (t, 0))] * 2,
            out_specs=[pl.BlockSpec((size, columns), lambda t, c: (t, 0))] * 2,
        ),
        out_shape=[jax.ShapeDtypeStruct((rows // 2, columns), BF16)] * 2,
        compiler_params=params(),
        cost_estimate=CHEAP,
        name=name,
    )(index.reshape(1), mine, theirs)


def add_parts(first, mine, theirs, n_y, name):
    rows, columns = mine.shape
    size = rows // n_y

    def body(first_ref, a_ref, b_ref, *outs):
        value = (a_ref[...].astype(F32) + b_ref[...].astype(F32)).astype(BF16)
        for i in range(n_y):

            @pl.when(pl.program_id(0) == i)
            def _():
                outs[i][...] = value

    block = pl.BlockSpec((size, columns), lambda s, c: ((c[0] + n_y - s) % n_y, 0))
    return pl.pallas_call(
        body,
        grid_spec=pltpu.PrefetchScalarGridSpec(
            num_scalar_prefetch=1,
            grid=(n_y,),
            in_specs=[block, block],
            out_specs=[pl.BlockSpec((size, columns), lambda s, c: (0, 0))] * n_y,
        ),
        out_shape=[jax.ShapeDtypeStruct((size, columns), BF16)] * n_y,
        compiler_params=params(),
        cost_estimate=CHEAP,
        name=name,
    )(first.reshape(1), mine, theirs)


def rotate_back(part_a, part_b, right, lower, upper, after, name):
    rows = part_a.shape[0]
    split = BLOCKS_B * BLOCK
    size = right.shape[1] - split
    tile = rows // 2

    def body(r_ref, a_ref, b_ref, *refs):
        acc = dot(a_ref[...], r_ref[lower:upper, split:], ((1,), (1,)))
        acc = acc + dot(b_ref[...], r_ref[lower:upper, :split], ((1,), (1,)))
        refs[-1][...] = acc.astype(BF16)

    return pl.pallas_call(
        body,
        grid=(2,),
        in_specs=[
            pl.BlockSpec(right.shape, lambda t: (0, 0), pipeline_mode=pl.Buffered(1)),
            pl.BlockSpec((tile, size), lambda t: (t, 0)),
            pl.BlockSpec((tile, split), lambda t: (t, 0)),
        ]
        + [ANY] * len(after),
        out_specs=pl.BlockSpec((tile, upper - lower), lambda t: (t, 0)),
        out_shape=jax.ShapeDtypeStruct((rows, upper - lower), BF16),
        compiler_params=params(),
        cost_estimate=CHEAP,
        name=name,
    )(right, part_a, part_b, *after)


def update_rows(ids, basis, backs, slab, cost, after, name):
    n = ids.shape[0] - 1
    cuts = 1
    tile = slab // cuts
    depth, width = backs[0].shape
    once = pl.Buffered(1)

    def body(ids_ref, a_ref, b_ref, back_a, back_b, *refs):
        acc = dot(a_ref[...], back_a[...]) + dot(b_ref[...], back_b[...])
        refs[-1][...] = acc.astype(BF16)

    return pl.pallas_call(
        body,
        grid_spec=pltpu.PrefetchScalarGridSpec(
            num_scalar_prefetch=1,
            grid=(cuts * n,),
            in_specs=[
                pl.BlockSpec((tile, depth), lambda t, c: (c[1 + t // cuts] * cuts + t % cuts, c[0])),
                pl.BlockSpec((tile, depth), lambda t, c: (c[1 + t // cuts] * cuts + t % cuts, 1 - c[0])),
                pl.BlockSpec((depth, width), lambda t, c: (0, 0), pipeline_mode=once),
                pl.BlockSpec((depth, width), lambda t, c: (0, 0), pipeline_mode=once),
            ]
            + [ANY] * len(after),
            out_specs=pl.BlockSpec((tile, width), lambda t, c: (t, 0)),
        ),
        out_shape=jax.ShapeDtypeStruct((n * slab, width), BF16),
        compiler_params=params(),
        cost_estimate=cost,
        name=name,
    )(ids.astype(jnp.int32), basis, basis, *backs, *after)


def on_device(
    gradients,
    left_basis,
    right_basis,
    first_moment,
    second_moment,
    omega_left,
    omega_right,
    sketch_left,
    sketch_right,
):
    n_row, n_col, n_dp = lax.axis_size("row"), lax.axis_size("col"), lax.axis_size("dp")
    row, col, dp = lax.axis_index("row"), lax.axis_index("col"), lax.axis_index("dp")
    y, z_lo, core = col // 4, (col // 2) % 2, col % 2
    n_y = n_col // 4
    own_grad = gradients[0]
    slab, width = own_grad.shape
    rows = slab * n_row
    k_dim = omega_left.shape[1]
    share = rows // n_col
    span = right_basis.shape[1]
    part = slab // n_col
    half = slab // 2

    every = (slice(None), slice(None))
    source_rows = [(row + n_row - s) % n_row for s in (0, 1, 3, 2)]

    most = slab // 2
    others = [swap_dp(own_grad[:most]), swap_dp(own_grad[most:])]
    came = {0: left_basis}
    for s in (1, 3, 2):
        came[s] = to_row(left_basis, s)

    omega_rows = lax.dynamic_slice_in_dim(omega_left, row * slab, slab, 0)
    summed = sum_replicas(own_grad, others, omega_rows, "sum_replicas")
    before, behind = to_row(summed, 1), to_row(summed, 3)
    middle = summed.shape[0] // 2
    on, back = to_row(before[:middle], 1), to_row(behind[middle:], 3)
    probe_left = 0.0
    for block, lower in ((summed, slab), (before, slab), (behind, slab), (back, slab - middle)):
        probe_left = probe_left + block[lower:].astype(F32)
    probe_left = probe_left.astype(BF16)

    pieces = []
    for c in range(2):
        for s in range(n_row):
            for z in range(2):
                source, target = (2 * z + c) * share, ((c * n_row + s) * 2 + z) * share
                pieces.append(
                    (came[s], 0, share, slice(source, source + share), slice(target, target + share))
                )
    wide = place(pieces, [jnp.int32(0)] * len(pieces), (share, rows), (others[0],), "left_basis_rows")
    basis = lax.all_gather(wide, "col", axis=0, tiled=True)

    def by_y(x, axis):
        return jnp.roll(jnp.flip(x, axis), row - (n_y - 1), axis)

    def by_owner(terms):
        terms = terms.astype(BF16).reshape(n_y, 2, 2, part, k_dim).transpose(2, 0, 1, 3, 4)
        return by_y(terms, 1).reshape(n_col, part, k_dim)

    right_terms = dot(own_grad, omega_right)
    left_terms = dot(own_grad, probe_left, ((1,), (1,)))
    extra = jnp.concatenate([by_owner(right_terms), by_owner(left_terms)], 1)
    extra = jnp.pad(extra, ((0, 0), (0, share - 2 * part), (0, 0))).reshape(-1, k_dim)
    total = place(
        [
            (summed, 0, slab, *every),
            (before, 0, slab, *every),
            (behind, 0, slab, *every),
            (on, 0, middle, *every),
            (back, 0, slab - middle, *every),
        ],
        [i * slab for i in source_rows] + [source_rows[3] * slab + middle],
        (rows, width),
        (extra,),
        "summed_gradient",
    )

    first = (row - y + n_y) % n_y
    left_theirs, sent_b = rotate(
        1 - core, basis, total, right_basis, extra, (), "rotate_theirs_b"
    )
    other_b = swap_core(sent_b)
    left_mine, mine_b = rotate(
        core, basis, total, right_basis, extra, (sent_b,), "rotate_mine_b"
    )
    keep_b, sent_b = split_parts(z_lo, mine_b, other_b, n_y, "pair_b")
    came_b = swap_z(sent_b)
    sent_a = rotate_rest(left_theirs, right_basis, (keep_b,), "rotate_theirs_a")
    other_a = swap_core(sent_a)
    mine_a = rotate_rest(left_mine, right_basis, (sent_a,), "rotate_mine_a")
    parts_a = add_parts(first, mine_a, other_a, n_y, "pair_a")
    came_a = [to_y(parts_a[s], s) for s in (1, 3, 2)]
    parts_b = add_parts(first, keep_b, came_b, n_y, "column_b")
    own_a, sent_a = sum_blocks(z_lo, [parts_a[0]] + came_a, (parts_b[0],), "column_a")
    came_a = swap_z(sent_a)
    own_b = parts_b[0].astype(F32)
    for s in (1, 3, 2):
        own_b = own_b + to_y(parts_b[s], s).astype(F32)
    own_a = own_a + came_a.astype(F32)

    split = BLOCKS_B * BLOCK
    firsts, seconds, directions = [], [], []
    for lower, upper, rotated in ((0, split, own_b[:, :split]), (split, span, own_a)):
        at = slice(lower, upper)
        first_part = 0.9 * first_moment[:, at] + 0.1 * rotated
        second_part = 0.95 * second_moment[:, at] + 0.05 * rotated * rotated
        directions.append((first_part / (jnp.sqrt(second_part) + 1e-08)).astype(BF16))
        firsts.append(first_part)
        seconds.append(second_part)
    first_new = jnp.concatenate(firsts, 1)
    second_new = jnp.concatenate(seconds, 1)
    sketches = own_b[:, split:]

    mine_b = jnp.concatenate([directions[0], sketches.astype(BF16)], 1)
    came_b = [mine_b] + [to_y(mine_b, s) for s in (1, 3, 2)]
    other = swap_z(directions[1])
    mine_a = jnp.where(
        z_lo == 0,
        jnp.concatenate([directions[1], other], 0),
        jnp.concatenate([other, directions[1]], 0),
    )
    came_a = [mine_a] + [to_y(mine_a, s) for s in (1, 3, 2)]
    order = [(first + s) % n_y for s in (0, 1, 3, 2)]
    near_b = place(
        [(x, 0, share, *every) for x in came_b],
        [i * share for i in order],
        (n_y * share, mine_b.shape[1]),
        (mine_a,),
        "direction_near_b",
    )
    far_b = swap_z(near_b)
    pieces = [(x, s * share, share, *every) for x in (near_b, far_b) for s in range(n_y)]
    starts = [2 * s * share + z * share for z in (z_lo, 1 - z_lo) for s in range(n_y)]
    own_b = place(pieces, starts, (2 * n_y * share, mine_b.shape[1]), (), "direction_b")
    own_a = place(
        [(x, 0, 2 * share, *every) for x in came_a],
        [i * 2 * share for i in order],
        (2 * n_y * share, span - split),
        (own_b,),
        "direction_a",
    )
    other_a, other_b = swap_core(own_a), swap_core(own_b)
    probes = [
        by_y(p[:, split:].reshape(n_y, 2, share, k_dim)[:, :, :part], 0) for p in (own_b, other_b)
    ]
    probes = jnp.where(core == 0, jnp.stack(probes, 2), jnp.stack(probes[::-1], 2))
    right_part = probe(own_grad, probes.reshape(slab, k_dim), (own_a,), "right_terms")
    right_came = [to_row(right_part, s) for s in (1, 3, 2)]

    slabs = [(row + s) % n_row for s in range(n_row)]
    far_ids, near_ids = jnp.stack([core] + slabs[1:]), jnp.stack([core] + slabs[:1])
    cut = width * 4 // 7
    sets = ((0, cut), (cut, width))
    backs = [[], []]
    after = (right_part,)
    for part_a, part_b, name in ((own_a, own_b, "own"), (other_a, other_b, "other")):
        for i, (lower, upper) in enumerate(sets):
            if i == 1:
                break
            backs[i].append(
                rotate_back(part_a, part_b, right_basis, lower, upper, after, f"back_{name}_{i}")
            )
            after = (backs[i][-1],)
    kept, sent = sum_blocks(dp, [right_part] + right_came, (backs[0][1],), "right_row_sum")
    kept = kept.astype(BF16)
    right_mine = jnp.where(
        dp == 0, jnp.concatenate([kept, sent], 0), jnp.concatenate([sent, kept], 0)
    )
    far_0 = update_rows(far_ids, basis, backs[0], slab, CHEAP, (sent,), "update_far_0")
    came_0 = [to_row(far_0[(s - 1) * slab : s * slab], s) for s in (2, 1, 3)]
    backs[1].append(
        rotate_back(own_a, own_b, right_basis, *sets[1], (far_0,), "back_own_1")
    )
    backs[1].append(
        rotate_back(other_a, other_b, right_basis, *sets[1], (backs[1][0],), "back_other_1")
    )
    far_1 = update_rows(far_ids, basis, backs[1], slab, CHEAP, (), "update_far_1")
    came_1 = [to_row(far_1[(s - 1) * slab : s * slab], s) for s in (2, 1, 3)]
    near_0 = update_rows(near_ids, basis, backs[0], slab, CHEAP, (far_1,), "update_near_0")

    own_0, sent = sum_blocks(dp, [near_0] + came_0, (), "update_sum_0")
    update_0 = (own_0 + swap_dp(sent).astype(F32)).astype(BF16)
    near_1 = update_rows(near_ids, basis, backs[1], slab, HEAVY, (sent,), "update_near_1")
    own_1, sent = sum_blocks(dp, [near_1] + came_1, (), "update_sum_1")
    update_1 = (own_1 + swap_dp(sent).astype(F32)).astype(BF16)
    update = jnp.concatenate([update_0, update_1], 1)

    right_sum = sum_pair(right_mine, swap_dp(right_mine), 1.0, (near_1,), "right_sum").astype(F32)
    right_new = 0.5 * sketch_right + 0.5 * right_sum / (n_dp * math.sqrt(rows))

    lines = part // n_dp
    left_mine = lax.dynamic_slice_in_dim(sketches, part + dp * lines, lines, 0)
    left_sent = lax.dynamic_slice_in_dim(sketches, part + (1 - dp) * lines, lines, 0)
    left_sent = jnp.pad(left_sent, ((0, 32 - lines), (0, 0))).astype(BF16)
    left_sent = sum_pair(left_sent, left_sent, 0.5, (near_1,), "left_sent")
    left_sum = left_mine + swap_dp(left_sent)[:lines].astype(F32)
    f_dim = width * n_col
    left_new = 0.5 * sketch_left + 0.5 * left_sum / (n_dp * math.sqrt(f_dim))

    return (
        update,
        first_new,
        second_new,
        left_new,
        right_new,
    )


def solution(mesh):
    return jax.shard_map(
        on_device,
        mesh=mesh,
        in_specs=(
            P("dp", "row", "col"),
            P("col", "row"),
            P("col", ("row", "dp")),
            P("col", ("row", "dp")),
            P("col", ("row", "dp")),
            P(),
            P("col", None),
            P(("row", "col", "dp"), None),
            P("col", None),
        ),
        out_specs=(
            P(("row", "dp"), "col"),
            P("col", ("row", "dp")),
            P("col", ("row", "dp")),
            P(("row", "col", "dp"), None),
            P("col", None),
        ),
        check_vma=False,
    )
```

```python
import math

import jax
import jax.numpy as jnp
from jax import lax
from jax.experimental import pallas as pl
from jax.experimental.pallas import tpu as pltpu
from jax.sharding import PartitionSpec as P

BF16 = jnp.bfloat16
F32 = jnp.float32


def dot(a, b, dims=((1,), (0,))):
    return lax.dot_general(a, b, (dims, ((), ())), preferred_element_type=F32)


def move(x, axis, target):
    n = lax.axis_size(axis)
    return lax.ppermute(x, axis, [(i, target(i) % n) for i in range(n)])


def swap_dp(x):
    return move(x, "dp", lambda i: i ^ 1)


def swap_core(x):
    return move(x, "col", lambda i: i ^ 1)


def swap_z(x):
    return move(x, "col", lambda i: i ^ 2)


def to_row(x, s):
    return move(x, "row", lambda i: i + s)


def to_y(x, s):
    return move(x, "col", lambda i: i + 4 * s)


def params():
    return pltpu.CompilerParams(vmem_limit_bytes=40 * 2**20)


BLOCK = 256
BLOCKS_B = 3
CHEAP = pl.CostEstimate(flops=1000, bytes_accessed=1000, transcendentals=0)
HEAVY = pl.CostEstimate(flops=10**11, bytes_accessed=10**8, transcendentals=0)
ANY = pl.BlockSpec(memory_space=pl.ANY)


def whole(x):
    return pl.BlockSpec(x.shape, lambda t, *c: (0,) * x.ndim)


def sum_replicas(grad, a, b, omega, after, name):
    rows, columns = a.shape
    k_dim = omega.shape[1]

    def body(grad_ref, omega_ref, a_ref, b_ref, *refs):
        out = refs[-1]
        out[:rows, :] = (a_ref[...].astype(F32) + b_ref[...].astype(F32)).astype(BF16)
        out[rows:, :] = dot(omega_ref[...], grad_ref[...], ((0,), (0,))).astype(BF16)

    return pl.pallas_call(
        body,
        grid=(1,),
        in_specs=[whole(grad), whole(omega), whole(a), whole(b)] + [ANY] * len(after),
        out_specs=pl.BlockSpec((rows + k_dim, columns), lambda t: (0, 0)),
        out_shape=jax.ShapeDtypeStruct((rows + k_dim, columns), BF16),
        compiler_params=params(),
        cost_estimate=CHEAP,
        name=name,
    )(grad, omega, a, b, *after)


def sum_pair(a, b, scale, after, name):
    def body(a_ref, b_ref, *refs):
        refs[-1][...] = (scale * (a_ref[...].astype(F32) + b_ref[...].astype(F32))).astype(BF16)

    return pl.pallas_call(
        body,
        grid=(1,),
        in_specs=[whole(a), whole(b)] + [ANY] * len(after),
        out_specs=whole(a),
        out_shape=jax.ShapeDtypeStruct(a.shape, BF16),
        compiler_params=params(),
        cost_estimate=CHEAP,
        name=name,
    )(a, b, *after)


def sum_blocks(index, blocks, after, name):
    n = len(blocks)
    rows, columns = blocks[0].shape
    size = rows // 2

    def body(index_ref, *refs):
        keep, send = refs[-2:]
        for out, lower in ((keep, index_ref[0] * size), (send, (1 - index_ref[0]) * size)):
            lower = pl.multiple_of(lower, 16)
            acc = refs[0][pl.ds(lower, size), :].astype(F32)
            for ref in refs[1:n]:
                acc = acc + ref[pl.ds(lower, size), :].astype(F32)
            out[...] = acc.astype(out.dtype)

    return pl.pallas_call(
        body,
        grid_spec=pltpu.PrefetchScalarGridSpec(
            num_scalar_prefetch=1,
            grid=(1,),
            in_specs=[whole(b) for b in blocks] + [ANY] * len(after),
            out_specs=[pl.BlockSpec((size, columns), lambda t, c: (0, 0))] * 2,
        ),
        out_shape=[
            jax.ShapeDtypeStruct((size, columns), F32),
            jax.ShapeDtypeStruct((size, columns), BF16),
        ],
        compiler_params=params(),
        cost_estimate=CHEAP,
        name=name,
    )(index.reshape(1), *blocks, *after)


def place(pieces, starts, shape, after, name):
    dtype = pieces[0][0].dtype
    arrays = []
    for piece in pieces:
        if not any(piece[0] is x for x in arrays):
            arrays.append(piece[0])
    where = [[x is piece[0] for x in arrays].index(True) for piece in pieces]

    def body(starts_ref, *refs):
        out = refs[-1]
        for i, (_, lower, count, source, target) in enumerate(pieces):
            start = pl.multiple_of(starts_ref[i], 16)
            out[pl.ds(start, count), target] = refs[where[i]][lower : lower + count, source]

    once = pl.Buffered(1)
    return pl.pallas_call(
        body,
        grid_spec=pltpu.PrefetchScalarGridSpec(
            num_scalar_prefetch=1,
            grid=(1,),
            in_specs=[
                pl.BlockSpec(x.shape, lambda t, c: (0, 0), pipeline_mode=once) for x in arrays
            ]
            + [ANY] * len(after),
            out_specs=pl.BlockSpec(shape, lambda t, c: (0, 0), pipeline_mode=once),
        ),
        out_shape=jax.ShapeDtypeStruct(shape, dtype),
        compiler_params=params(),
        cost_estimate=CHEAP,
        name=name,
    )(jnp.stack(starts).astype(jnp.int32), *arrays, *after)


def probe(grad, omega, after, name):
    size = (grad.shape[1], omega.shape[1])

    def body(g_ref, o_ref, *refs):
        refs[-1][...] = dot(g_ref[...], o_ref[...], ((0,), (0,))).astype(BF16)

    return pl.pallas_call(
        body,
        grid=(1,),
        in_specs=[whole(grad), whole(omega)] + [ANY] * len(after),
        out_specs=pl.BlockSpec(size, lambda t: (0, 0)),
        out_shape=jax.ShapeDtypeStruct(size, BF16),
        compiler_params=params(),
        cost_estimate=CHEAP,
        name=name,
    )(grad, omega, *after)


def rotate(index, basis, total, right, extra, after, name):
    rows, width = total.shape
    size = basis.shape[1] // 2
    span = BLOCKS_B * BLOCK
    wide = span + extra.shape[1]
    tiles = 2
    tile = size // tiles
    once = pl.Buffered(1)

    def body(index_ref, basis_ref, total_ref, extra_ref, *refs):
        left_out, out = refs[-2:]
        left = (0.5 * dot(basis_ref[...], total_ref[...], ((0,), (0,)))).astype(BF16)
        left_out[...] = left
        for i in range(BLOCKS_B):
            at = slice(i * BLOCK, (i + 1) * BLOCK)
            out[:, at] = dot(left, refs[i][...]).astype(BF16)
        out[:, span:] = extra_ref[...]

    return pl.pallas_call(
        body,
        grid_spec=pltpu.PrefetchScalarGridSpec(
            num_scalar_prefetch=1,
            grid=(tiles,),
            in_specs=[
                pl.BlockSpec((rows, tile), lambda t, c: (0, c[0] * tiles + t)),
                pl.BlockSpec((rows, width), lambda t, c: (0, 0), pipeline_mode=once),
                pl.BlockSpec((tile, extra.shape[1]), lambda t, c: (c[0] * tiles + t, 0)),
            ]
            + [
                pl.BlockSpec((width, BLOCK), lambda t, c, i=i: (0, i), pipeline_mode=once)
                for i in range(BLOCKS_B)
            ]
            + [ANY] * len(after),
            out_specs=[
                pl.BlockSpec((tile, width), lambda t, c: (t, 0)),
                pl.BlockSpec((tile, wide), lambda t, c: (t, 0)),
            ],
        ),
        out_shape=[
            jax.ShapeDtypeStruct((size, width), BF16),
            jax.ShapeDtypeStruct((size, wide), BF16),
        ],
        compiler_params=params(),
        cost_estimate=CHEAP,
        name=name,
    )(index.reshape(1), basis, total, extra, *[right] * BLOCKS_B, *after)


def rotate_rest(left, right, after, name):
    rows, width = left.shape
    n = right.shape[1] // BLOCK - BLOCKS_B
    span = n * BLOCK
    tile = rows // 2

    def body(left_ref, *refs):
        for i in range(n):
            at = slice(i * BLOCK, (i + 1) * BLOCK)
            refs[-1][:, at] = dot(left_ref[...], refs[i][...]).astype(BF16)

    return pl.pallas_call(
        body,
        grid=(2,),
        in_specs=[
            pl.BlockSpec((tile, width), lambda t: (t, 0)),
        ]
        + [
            pl.BlockSpec(
                (width, BLOCK), lambda t, i=i: (0, BLOCKS_B + i), pipeline_mode=pl.Buffered(1)
            )
            for i in range(n)
        ]
        + [ANY] * len(after),
        out_specs=pl.BlockSpec((tile, span), lambda t: (t, 0)),
        out_shape=jax.ShapeDtypeStruct((rows, span), BF16),
        compiler_params=params(),
        cost_estimate=CHEAP,
        name=name,
    )(left, *[right] * n, *after)


def split_parts(index, mine, theirs, n_y, name):
    rows, columns = mine.shape
    size = rows // n_y // 2

    def body(index_ref, a_ref, b_ref, keep, send):
        for out, lower in ((keep, index_ref[0] * size), (send, (1 - index_ref[0]) * size)):
            at = pl.ds(pl.multiple_of(lower, 16), size)
            out[...] = (a_ref[at, :].astype(F32) + b_ref[at, :].astype(F32)).astype(BF16)

    return pl.pallas_call(
        body,
        grid_spec=pltpu.PrefetchScalarGridSpec(
            num_scalar_prefetch=1,
            grid=(n_y,),
            in_specs=[pl.BlockSpec((2 * size, columns), lambda t, c: (t, 0))] * 2,
            out_specs=[pl.BlockSpec((size, columns), lambda t, c: (t, 0))] * 2,
        ),
        out_shape=[jax.ShapeDtypeStruct((rows // 2, columns), BF16)] * 2,
        compiler_params=params(),
        cost_estimate=CHEAP,
        name=name,
    )(index.reshape(1), mine, theirs)


def add_parts(first, mine, theirs, n_y, after, name):
    rows, columns = mine.shape
    size = rows // n_y

    def body(first_ref, a_ref, b_ref, *refs):
        outs = refs[len(after) :]
        value = (a_ref[...].astype(F32) + b_ref[...].astype(F32)).astype(BF16)
        for i in range(n_y):

            @pl.when(pl.program_id(0) == i)
            def _():
                outs[i][...] = value

    block = pl.BlockSpec((size, columns), lambda s, c: ((c[0] + n_y - s) % n_y, 0))
    return pl.pallas_call(
        body,
        grid_spec=pltpu.PrefetchScalarGridSpec(
            num_scalar_prefetch=1,
            grid=(n_y,),
            in_specs=[block, block] + [ANY] * len(after),
            out_specs=[pl.BlockSpec((size, columns), lambda s, c: (0, 0))] * n_y,
        ),
        out_shape=[jax.ShapeDtypeStruct((size, columns), BF16)] * n_y,
        compiler_params=params(),
        cost_estimate=CHEAP,
        name=name,
    )(first.reshape(1), mine, theirs, *after)


def rotate_back(part_a, part_b, right, lower, upper, after, name):
    rows = part_a.shape[0]
    split = BLOCKS_B * BLOCK
    size = right.shape[1] - split
    tile = rows // 2

    def body(r_ref, a_ref, b_ref, *refs):
        acc = dot(a_ref[...], r_ref[lower:upper, split:], ((1,), (1,)))
        acc = acc + dot(b_ref[...], r_ref[lower:upper, :split], ((1,), (1,)))
        refs[-1][...] = acc.astype(BF16)

    return pl.pallas_call(
        body,
        grid=(2,),
        in_specs=[
            pl.BlockSpec(right.shape, lambda t: (0, 0), pipeline_mode=pl.Buffered(1)),
            pl.BlockSpec((tile, size), lambda t: (t, 0)),
            pl.BlockSpec((tile, split), lambda t: (t, 0)),
        ]
        + [ANY] * len(after),
        out_specs=pl.BlockSpec((tile, upper - lower), lambda t: (t, 0)),
        out_shape=jax.ShapeDtypeStruct((rows, upper - lower), BF16),
        compiler_params=params(),
        cost_estimate=CHEAP,
        name=name,
    )(right, part_a, part_b, *after)


def update_rows(ids, basis, backs, slab, cost, after, name):
    n = ids.shape[0] - 1
    cuts = 1
    tile = slab // cuts
    depth, width = backs[0].shape
    once = pl.Buffered(1)

    def body(ids_ref, a_ref, b_ref, back_a, back_b, *refs):
        acc = dot(a_ref[...], back_a[...]) + dot(b_ref[...], back_b[...])
        refs[-1][...] = acc.astype(BF16)

    return pl.pallas_call(
        body,
        grid_spec=pltpu.PrefetchScalarGridSpec(
            num_scalar_prefetch=1,
            grid=(cuts * n,),
            in_specs=[
                pl.BlockSpec((tile, depth), lambda t, c: (c[1 + t // cuts] * cuts + t % cuts, c[0])),
                pl.BlockSpec((tile, depth), lambda t, c: (c[1 + t // cuts] * cuts + t % cuts, 1 - c[0])),
                pl.BlockSpec((depth, width), lambda t, c: (0, 0), pipeline_mode=once),
                pl.BlockSpec((depth, width), lambda t, c: (0, 0), pipeline_mode=once),
            ]
            + [ANY] * len(after),
            out_specs=pl.BlockSpec((tile, width), lambda t, c: (t, 0)),
        ),
        out_shape=jax.ShapeDtypeStruct((n * slab, width), BF16),
        compiler_params=params(),
        cost_estimate=cost,
        name=name,
    )(ids.astype(jnp.int32), basis, basis, *backs, *after)


def on_device(
    gradients,
    left_basis,
    right_basis,
    first_moment,
    second_moment,
    omega_left,
    omega_right,
    sketch_left,
    sketch_right,
):
    n_row, n_col, n_dp = lax.axis_size("row"), lax.axis_size("col"), lax.axis_size("dp")
    row, col, dp = lax.axis_index("row"), lax.axis_index("col"), lax.axis_index("dp")
    y, z_lo, core = col // 4, (col // 2) % 2, col % 2
    n_y = n_col // 4
    own_grad = gradients[0]
    slab, width = own_grad.shape
    rows = slab * n_row
    k_dim = omega_left.shape[1]
    share = rows // n_col
    span = right_basis.shape[1]
    part = slab // n_col
    half = slab // 2

    every = (slice(None), slice(None))
    source_rows = [(row + n_row - s) % n_row for s in (0, 1, 3, 2)]

    came = {0: left_basis}
    for s in (1, 3, 2):
        came[s] = to_row(left_basis, s)
    tops = [own_grad[:half], own_grad[half:]]
    others = [swap_dp(x) for x in tops]

    pieces = []
    for c in range(2):
        for s in range(n_row):
            for z in range(2):
                source, target = (2 * z + c) * share, ((c * n_row + s) * 2 + z) * share
                pieces.append(
                    (came[s], 0, share, slice(source, source + share), slice(target, target + share))
                )
    wide = place(pieces, [jnp.int32(0)] * len(pieces), (share, rows), (others[0],), "left_basis_rows")
    basis = lax.all_gather(wide, "col", axis=0, tiled=True)

    omega_rows = lax.dynamic_slice_in_dim(omega_left, row * slab, slab, 0)
    total_pieces, total_starts = [], []
    probe_left = 0.0
    after = (wide,)
    for h in range(2):
        if h == 0:
            summed = sum_pair(tops[0], others[0], 1.0, after, "sum_replicas_0")
        else:
            summed = sum_replicas(own_grad, tops[1], others[1], omega_rows, after, "sum_replicas_1")
        middle = summed.shape[0] // 2
        before, behind = to_row(summed, 1), to_row(summed, 3)
        after = (before, behind)
        on, back = to_row(before[:middle], 1), to_row(behind[middle:], 3)
        for block, count, i, skip in (
            (summed, half, 0, 0),
            (before, half, 1, 0),
            (behind, half, 2, 0),
            (on, middle, 3, 0),
            (back, half - middle, 3, middle),
        ):
            total_pieces.append((block, 0, count, *every))
            total_starts.append(source_rows[i] * slab + h * half + skip)
            if h == 1 and count != middle:
                probe_left = probe_left + block[count:].astype(F32)
    probe_left = probe_left.astype(BF16)
    right_terms = dot(own_grad, omega_right)

    def by_y(x, axis):
        return jnp.roll(jnp.flip(x, axis), row - (n_y - 1), axis)

    def by_owner(terms):
        terms = terms.astype(BF16).reshape(n_y, 2, 2, part, k_dim).transpose(2, 0, 1, 3, 4)
        return by_y(terms, 1).reshape(n_col, part, k_dim)

    left_terms = dot(own_grad, probe_left, ((1,), (1,)))
    extra = jnp.concatenate([by_owner(right_terms), by_owner(left_terms)], 1)
    extra = jnp.pad(extra, ((0, 0), (0, share - 2 * part), (0, 0))).reshape(-1, k_dim)
    total = place(total_pieces, total_starts, (rows, width), (extra,), "summed_gradient")

    first = (row - y + n_y) % n_y
    left_theirs, sent_b = rotate(
        1 - core, basis, total, right_basis, extra, (), "rotate_theirs_b"
    )
    other_b = swap_core(sent_b)
    left_mine, mine_b = rotate(
        core, basis, total, right_basis, extra, (sent_b,), "rotate_mine_b"
    )
    keep_b, sent_b = split_parts(z_lo, mine_b, other_b, n_y, "pair_b")
    came_b = swap_z(sent_b)
    sent_a = rotate_rest(left_theirs, right_basis, (keep_b,), "rotate_theirs_a")
    other_a = swap_core(sent_a)
    mine_a = rotate_rest(left_mine, right_basis, (sent_a,), "rotate_mine_a")
    parts_a = add_parts(first, mine_a, other_a, n_y, (), "pair_a")
    came_a = [to_y(parts_a[s], s) for s in (1, 3, 2)]
    parts_b = add_parts(first, keep_b, came_b, n_y, (parts_a[0],), "column_b")
    own_a, sent_a = sum_blocks(z_lo, [parts_a[0]] + came_a, (parts_b[0],), "column_a")
    came_a = swap_z(sent_a)
    own_b = parts_b[0].astype(F32)
    for s in (1, 3, 2):
        own_b = own_b + to_y(parts_b[s], s).astype(F32)
    own_a = own_a + came_a.astype(F32)

    split = BLOCKS_B * BLOCK
    firsts, seconds, directions = [], [], []
    for lower, upper, rotated in ((0, split, own_b[:, :split]), (split, span, own_a)):
        at = slice(lower, upper)
        first_part = 0.9 * first_moment[:, at] + 0.1 * rotated
        second_part = 0.95 * second_moment[:, at] + 0.05 * rotated * rotated
        directions.append((first_part / (jnp.sqrt(second_part) + 1e-08)).astype(BF16))
        firsts.append(first_part)
        seconds.append(second_part)
    first_new = jnp.concatenate(firsts, 1)
    second_new = jnp.concatenate(seconds, 1)
    sketches = own_b[:, split:]

    mine_b = jnp.concatenate([directions[0], sketches.astype(BF16)], 1)
    came_b = [mine_b] + [to_y(mine_b, s) for s in (1, 3, 2)]
    other = swap_z(directions[1])
    mine_a = jnp.where(
        z_lo == 0,
        jnp.concatenate([directions[1], other], 0),
        jnp.concatenate([other, directions[1]], 0),
    )
    came_a = [mine_a] + [to_y(mine_a, s) for s in (1, 3, 2)]
    order = [(first + s) % n_y for s in (0, 1, 3, 2)]
    near_b = place(
        [(x, 0, share, *every) for x in came_b],
        [i * share for i in order],
        (n_y * share, mine_b.shape[1]),
        (mine_a,),
        "direction_near_b",
    )
    far_b = swap_z(near_b)
    pieces = [(x, s * share, share, *every) for x in (near_b, far_b) for s in range(n_y)]
    starts = [2 * s * share + z * share for z in (z_lo, 1 - z_lo) for s in range(n_y)]
    own_b = place(pieces, starts, (2 * n_y * share, mine_b.shape[1]), (), "direction_b")
    own_a = place(
        [(x, 0, 2 * share, *every) for x in came_a],
        [i * 2 * share for i in order],
        (2 * n_y * share, span - split),
        (own_b,),
        "direction_a",
    )
    other_a, other_b = swap_core(own_a), swap_core(own_b)
    probes = [
        by_y(p[:, split:].reshape(n_y, 2, share, k_dim)[:, :, :part], 0) for p in (own_b, other_b)
    ]
    probes = jnp.where(core == 0, jnp.stack(probes, 2), jnp.stack(probes[::-1], 2))
    right_part = probe(own_grad, probes.reshape(slab, k_dim), (own_a,), "right_terms")
    right_came = [to_row(right_part, s) for s in (1, 3, 2)]

    slabs = [(row + s) % n_row for s in range(n_row)]
    far_ids, near_ids = jnp.stack([core] + slabs[1:]), jnp.stack([core] + slabs[:1])
    cut = width * 4 // 7
    sets = ((0, cut), (cut, width))
    backs = [[], []]
    after = (right_part,)
    for part_a, part_b, name in ((own_a, own_b, "own"), (other_a, other_b, "other")):
        for i, (lower, upper) in enumerate(sets):
            if i == 1:
                break
            backs[i].append(
                rotate_back(part_a, part_b, right_basis, lower, upper, after, f"back_{name}_{i}")
            )
            after = (backs[i][-1],)
    kept, sent = sum_blocks(dp, [right_part] + right_came, (backs[0][1],), "right_row_sum")
    kept = kept.astype(BF16)
    right_mine = jnp.where(
        dp == 0, jnp.concatenate([kept, sent], 0), jnp.concatenate([sent, kept], 0)
    )
    far_0 = update_rows(far_ids, basis, backs[0], slab, CHEAP, (sent,), "update_far_0")
    came_0 = [to_row(far_0[(s - 1) * slab : s * slab], s) for s in (2, 1, 3)]
    backs[1].append(
        rotate_back(own_a, own_b, right_basis, *sets[1], (far_0,), "back_own_1")
    )
    backs[1].append(
        rotate_back(other_a, other_b, right_basis, *sets[1], (backs[1][0],), "back_other_1")
    )
    far_1 = update_rows(far_ids, basis, backs[1], slab, CHEAP, (), "update_far_1")
    came_1 = [to_row(far_1[(s - 1) * slab : s * slab], s) for s in (2, 1, 3)]
    near_0 = update_rows(near_ids, basis, backs[0], slab, CHEAP, (far_1,), "update_near_0")

    own_0, sent = sum_blocks(dp, [near_0] + came_0, (), "update_sum_0")
    update_0 = (own_0 + swap_dp(sent).astype(F32)).astype(BF16)
    near_1 = update_rows(near_ids, basis, backs[1], slab, HEAVY, (sent,), "update_near_1")
    own_1, sent = sum_blocks(dp, [near_1] + came_1, (), "update_sum_1")
    update_1 = (own_1 + swap_dp(sent).astype(F32)).astype(BF16)
    update = jnp.concatenate([update_0, update_1], 1)

    right_sum = sum_pair(right_mine, swap_dp(right_mine), 1.0, (near_1,), "right_sum").astype(F32)
    right_new = 0.5 * sketch_right + 0.5 * right_sum / (n_dp * math.sqrt(rows))

    lines = part // n_dp
    left_mine = lax.dynamic_slice_in_dim(sketches, part + dp * lines, lines, 0)
    left_sent = lax.dynamic_slice_in_dim(sketches, part + (1 - dp) * lines, lines, 0)
    left_sent = jnp.pad(left_sent, ((0, 32 - lines), (0, 0))).astype(BF16)
    left_sent = sum_pair(left_sent, left_sent, 0.5, (near_1,), "left_sent")
    left_sum = left_mine + swap_dp(left_sent)[:lines].astype(F32)
    f_dim = width * n_col
    left_new = 0.5 * sketch_left + 0.5 * left_sum / (n_dp * math.sqrt(f_dim))

    return (
        update,
        first_new,
        second_new,
        left_new,
        right_new,
    )


def solution(mesh):
    return jax.shard_map(
        on_device,
        mesh=mesh,
        in_specs=(
            P("dp", "row", "col"),
            P("col", "row"),
            P("col", ("row", "dp")),
            P("col", ("row", "dp")),
            P("col", ("row", "dp")),
            P(),
            P("col", None),
            P(("row", "col", "dp"), None),
            P("col", None),
        ),
        out_specs=(
            P(("row", "dp"), "col"),
            P("col", ("row", "dp")),
            P("col", ("row", "dp")),
            P(("row", "col", "dp"), None),
            P("col", None),
        ),
        check_vma=False,
    )
```

```python
import math

import jax
import jax.numpy as jnp
from jax import lax
from jax.experimental import pallas as pl
from jax.experimental.pallas import tpu as pltpu
from jax.sharding import PartitionSpec as P

BF16 = jnp.bfloat16
F32 = jnp.float32


def dot(a, b, dims=((1,), (0,))):
    return lax.dot_general(a, b, (dims, ((), ())), preferred_element_type=F32)


def move(x, axis, target):
    n = lax.axis_size(axis)
    return lax.ppermute(x, axis, [(i, target(i) % n) for i in range(n)])


def swap_dp(x):
    return move(x, "dp", lambda i: i ^ 1)


def swap_core(x):
    return move(x, "col", lambda i: i ^ 1)


def swap_z(x):
    return move(x, "col", lambda i: i ^ 2)


def to_row(x, s):
    return move(x, "row", lambda i: i + s)


def to_y(x, s):
    return move(x, "col", lambda i: i + 4 * s)


def params(mib=40):
    return pltpu.CompilerParams(vmem_limit_bytes=mib * 2**20)


BLOCK = 256
BLOCKS_B = 3
CHEAP = pl.CostEstimate(flops=1000, bytes_accessed=1000, transcendentals=0)
HEAVY = pl.CostEstimate(flops=10**11, bytes_accessed=10**8, transcendentals=0)
ANY = pl.BlockSpec(memory_space=pl.ANY)


def whole(x):
    return pl.BlockSpec(x.shape, lambda t, *c: (0,) * x.ndim)


def sum_replicas(grad, a, b, omega, after, name):
    rows, columns = a.shape
    k_dim = omega.shape[1]

    def body(grad_ref, omega_ref, a_ref, b_ref, *refs):
        out = refs[-1]
        out[:rows, :] = (a_ref[...].astype(F32) + b_ref[...].astype(F32)).astype(BF16)
        out[rows:, :] = dot(omega_ref[...], grad_ref[...], ((0,), (0,))).astype(BF16)

    return pl.pallas_call(
        body,
        grid=(1,),
        in_specs=[whole(grad), whole(omega), whole(a), whole(b)] + [ANY] * len(after),
        out_specs=pl.BlockSpec((rows + k_dim, columns), lambda t: (0, 0)),
        out_shape=jax.ShapeDtypeStruct((rows + k_dim, columns), BF16),
        compiler_params=params(),
        cost_estimate=CHEAP,
        name=name,
    )(grad, omega, a, b, *after)


def sum_pair(a, b, scale, after, name):
    def body(a_ref, b_ref, *refs):
        refs[-1][...] = (scale * (a_ref[...].astype(F32) + b_ref[...].astype(F32))).astype(BF16)

    return pl.pallas_call(
        body,
        grid=(1,),
        in_specs=[whole(a), whole(b)] + [ANY] * len(after),
        out_specs=whole(a),
        out_shape=jax.ShapeDtypeStruct(a.shape, BF16),
        compiler_params=params(),
        cost_estimate=CHEAP,
        name=name,
    )(a, b, *after)


def sum_blocks(index, blocks, after, name):
    n = len(blocks)
    rows, columns = blocks[0].shape
    size = rows // 2

    def body(index_ref, *refs):
        keep, send = refs[-2:]
        for out, lower in ((keep, index_ref[0] * size), (send, (1 - index_ref[0]) * size)):
            lower = pl.multiple_of(lower, 16)
            acc = refs[0][pl.ds(lower, size), :].astype(F32)
            for ref in refs[1:n]:
                acc = acc + ref[pl.ds(lower, size), :].astype(F32)
            out[...] = acc.astype(out.dtype)

    return pl.pallas_call(
        body,
        grid_spec=pltpu.PrefetchScalarGridSpec(
            num_scalar_prefetch=1,
            grid=(1,),
            in_specs=[whole(b) for b in blocks] + [ANY] * len(after),
            out_specs=[pl.BlockSpec((size, columns), lambda t, c: (0, 0))] * 2,
        ),
        out_shape=[
            jax.ShapeDtypeStruct((size, columns), F32),
            jax.ShapeDtypeStruct((size, columns), BF16),
        ],
        compiler_params=params(),
        cost_estimate=CHEAP,
        name=name,
    )(index.reshape(1), *blocks, *after)


def place(pieces, starts, shape, after, name):
    dtype = pieces[0][0].dtype
    arrays = []
    for piece in pieces:
        if not any(piece[0] is x for x in arrays):
            arrays.append(piece[0])
    where = [[x is piece[0] for x in arrays].index(True) for piece in pieces]

    def body(starts_ref, *refs):
        out = refs[-1]
        for i, (_, lower, count, source, target) in enumerate(pieces):
            start = pl.multiple_of(starts_ref[i], 16)
            out[pl.ds(start, count), target] = refs[where[i]][lower : lower + count, source]

    once = pl.Buffered(1)
    return pl.pallas_call(
        body,
        grid_spec=pltpu.PrefetchScalarGridSpec(
            num_scalar_prefetch=1,
            grid=(1,),
            in_specs=[
                pl.BlockSpec(x.shape, lambda t, c: (0, 0), pipeline_mode=once) for x in arrays
            ]
            + [ANY] * len(after),
            out_specs=pl.BlockSpec(shape, lambda t, c: (0, 0), pipeline_mode=once),
        ),
        out_shape=jax.ShapeDtypeStruct(shape, dtype),
        compiler_params=params(),
        cost_estimate=CHEAP,
        name=name,
    )(jnp.stack(starts).astype(jnp.int32), *arrays, *after)


def probe(grad, omega, after, name):
    size = (grad.shape[1], omega.shape[1])

    def body(g_ref, o_ref, *refs):
        refs[-1][...] = dot(g_ref[...], o_ref[...], ((0,), (0,))).astype(BF16)

    return pl.pallas_call(
        body,
        grid=(1,),
        in_specs=[whole(grad), whole(omega)] + [ANY] * len(after),
        out_specs=pl.BlockSpec(size, lambda t: (0, 0)),
        out_shape=jax.ShapeDtypeStruct(size, BF16),
        compiler_params=params(),
        cost_estimate=CHEAP,
        name=name,
    )(grad, omega, *after)


def rotate(index, basis, total, right, extra, after, name):
    rows, width = total.shape
    size = basis.shape[1] // 2
    span = BLOCKS_B * BLOCK
    wide = span + extra.shape[1]
    tiles = 2
    tile = size // tiles
    once = pl.Buffered(1)

    def body(index_ref, basis_ref, total_ref, extra_ref, *refs):
        left_out, out = refs[-2:]
        left = (0.5 * dot(basis_ref[...], total_ref[...], ((0,), (0,)))).astype(BF16)
        left_out[...] = left
        for i in range(BLOCKS_B):
            at = slice(i * BLOCK, (i + 1) * BLOCK)
            out[:, at] = dot(left, refs[i][...]).astype(BF16)
        out[:, span:] = extra_ref[...]

    return pl.pallas_call(
        body,
        grid_spec=pltpu.PrefetchScalarGridSpec(
            num_scalar_prefetch=1,
            grid=(tiles,),
            in_specs=[
                pl.BlockSpec((rows, tile), lambda t, c: (0, c[0] * tiles + t)),
                pl.BlockSpec((rows, width), lambda t, c: (0, 0), pipeline_mode=once),
                pl.BlockSpec((tile, extra.shape[1]), lambda t, c: (c[0] * tiles + t, 0)),
            ]
            + [
                pl.BlockSpec((width, BLOCK), lambda t, c, i=i: (0, i), pipeline_mode=once)
                for i in range(BLOCKS_B)
            ]
            + [ANY] * len(after),
            out_specs=[
                pl.BlockSpec((tile, width), lambda t, c: (t, 0)),
                pl.BlockSpec((tile, wide), lambda t, c: (t, 0)),
            ],
        ),
        out_shape=[
            jax.ShapeDtypeStruct((size, width), BF16),
            jax.ShapeDtypeStruct((size, wide), BF16),
        ],
        compiler_params=params(),
        cost_estimate=CHEAP,
        name=name,
    )(index.reshape(1), basis, total, extra, *[right] * BLOCKS_B, *after)


def rotate_rest(left, right, after, name):
    rows, width = left.shape
    n = right.shape[1] // BLOCK - BLOCKS_B
    span = n * BLOCK
    tile = rows // 2

    def body(left_ref, *refs):
        for i in range(n):
            at = slice(i * BLOCK, (i + 1) * BLOCK)
            refs[-1][:, at] = dot(left_ref[...], refs[i][...]).astype(BF16)

    return pl.pallas_call(
        body,
        grid=(2,),
        in_specs=[
            pl.BlockSpec((tile, width), lambda t: (t, 0)),
        ]
        + [
            pl.BlockSpec(
                (width, BLOCK), lambda t, i=i: (0, BLOCKS_B + i), pipeline_mode=pl.Buffered(1)
            )
            for i in range(n)
        ]
        + [ANY] * len(after),
        out_specs=pl.BlockSpec((tile, span), lambda t: (t, 0)),
        out_shape=jax.ShapeDtypeStruct((rows, span), BF16),
        compiler_params=params(),
        cost_estimate=CHEAP,
        name=name,
    )(left, *[right] * n, *after)


def rotate_rest_parts(first, left, right, theirs, n_y, after, name):
    rows, width = left.shape
    n = right.shape[1] // BLOCK - BLOCKS_B
    span = n * BLOCK
    size = rows // n_y

    def body(first_ref, left_ref, theirs_ref, *refs):
        outs = refs[len(refs) - n_y :]
        for j in range(n_y):

            @pl.when(pl.program_id(0) == j)
            def _():
                for i in range(n):
                    at = slice(i * BLOCK, (i + 1) * BLOCK)
                    value = dot(left_ref[...], refs[i][...]) + theirs_ref[:, at].astype(F32)
                    outs[j][:, at] = value.astype(BF16)

    pick = lambda t, c: ((c[0] + n_y - t) % n_y, 0)
    return pl.pallas_call(
        body,
        grid_spec=pltpu.PrefetchScalarGridSpec(
            num_scalar_prefetch=1,
            grid=(n_y,),
            in_specs=[pl.BlockSpec((size, width), pick), pl.BlockSpec((size, span), pick)]
            + [
                pl.BlockSpec(
                    (width, BLOCK), lambda t, c, i=i: (0, BLOCKS_B + i), pipeline_mode=pl.Buffered(1)
                )
                for i in range(n)
            ]
            + [ANY] * len(after),
            out_specs=[pl.BlockSpec((size, span), lambda t, c: (0, 0))] * n_y,
        ),
        out_shape=[jax.ShapeDtypeStruct((size, span), BF16)] * n_y,
        compiler_params=params(56),
        cost_estimate=CHEAP,
        name=name,
    )(first.reshape(1), left, theirs, *[right] * n, *after)


def split_parts(index, mine, theirs, n_y, after, name):
    rows, columns = mine.shape
    size = rows // n_y // 2

    def body(index_ref, a_ref, b_ref, *refs):
        keep, send = refs[-2:]
        for out, lower in ((keep, index_ref[0] * size), (send, (1 - index_ref[0]) * size)):
            at = pl.ds(pl.multiple_of(lower, 16), size)
            out[...] = (a_ref[at, :].astype(F32) + b_ref[at, :].astype(F32)).astype(BF16)

    return pl.pallas_call(
        body,
        grid_spec=pltpu.PrefetchScalarGridSpec(
            num_scalar_prefetch=1,
            grid=(n_y,),
            in_specs=[pl.BlockSpec((2 * size, columns), lambda t, c: (t, 0))] * 2 + [ANY] * len(after),
            out_specs=[pl.BlockSpec((size, columns), lambda t, c: (t, 0))] * 2,
        ),
        out_shape=[jax.ShapeDtypeStruct((rows // 2, columns), BF16)] * 2,
        compiler_params=params(),
        cost_estimate=CHEAP,
        name=name,
    )(index.reshape(1), mine, theirs, *after)


def add_parts(first, mine, theirs, n_y, after, name):
    rows, columns = mine.shape
    size = rows // n_y

    def body(first_ref, a_ref, b_ref, *refs):
        outs = refs[len(after) :]
        value = (a_ref[...].astype(F32) + b_ref[...].astype(F32)).astype(BF16)
        for i in range(n_y):

            @pl.when(pl.program_id(0) == i)
            def _():
                outs[i][...] = value

    block = pl.BlockSpec((size, columns), lambda s, c: ((c[0] + n_y - s) % n_y, 0))
    return pl.pallas_call(
        body,
        grid_spec=pltpu.PrefetchScalarGridSpec(
            num_scalar_prefetch=1,
            grid=(n_y,),
            in_specs=[block, block] + [ANY] * len(after),
            out_specs=[pl.BlockSpec((size, columns), lambda s, c: (0, 0))] * n_y,
        ),
        out_shape=[jax.ShapeDtypeStruct((size, columns), BF16)] * n_y,
        compiler_params=params(),
        cost_estimate=CHEAP,
        name=name,
    )(first.reshape(1), mine, theirs, *after)


def rotate_back(part_a, part_b, right, lower, upper, after, name):
    rows = part_a.shape[0]
    split = BLOCKS_B * BLOCK
    size = right.shape[1] - split
    tile = rows // 2

    def body(r_ref, a_ref, b_ref, *refs):
        acc = dot(a_ref[...], r_ref[lower:upper, split:], ((1,), (1,)))
        acc = acc + dot(b_ref[...], r_ref[lower:upper, :split], ((1,), (1,)))
        refs[-1][...] = acc.astype(BF16)

    return pl.pallas_call(
        body,
        grid=(2,),
        in_specs=[
            pl.BlockSpec(right.shape, lambda t: (0, 0), pipeline_mode=pl.Buffered(1)),
            pl.BlockSpec((tile, size), lambda t: (t, 0)),
            pl.BlockSpec((tile, split), lambda t: (t, 0)),
        ]
        + [ANY] * len(after),
        out_specs=pl.BlockSpec((tile, upper - lower), lambda t: (t, 0)),
        out_shape=jax.ShapeDtypeStruct((rows, upper - lower), BF16),
        compiler_params=params(),
        cost_estimate=CHEAP,
        name=name,
    )(right, part_a, part_b, *after)


def update_rows(ids, basis, backs, slab, cost, after, name):
    n = ids.shape[0] - 1
    cuts = 1
    tile = slab // cuts
    depth, width = backs[0].shape
    once = pl.Buffered(1)

    def body(ids_ref, a_ref, b_ref, back_a, back_b, *refs):
        acc = dot(a_ref[...], back_a[...]) + dot(b_ref[...], back_b[...])
        refs[-1][...] = acc.astype(BF16)

    return pl.pallas_call(
        body,
        grid_spec=pltpu.PrefetchScalarGridSpec(
            num_scalar_prefetch=1,
            grid=(cuts * n,),
            in_specs=[
                pl.BlockSpec((tile, depth), lambda t, c: (c[1 + t // cuts] * cuts + t % cuts, c[0])),
                pl.BlockSpec((tile, depth), lambda t, c: (c[1 + t // cuts] * cuts + t % cuts, 1 - c[0])),
                pl.BlockSpec((depth, width), lambda t, c: (0, 0), pipeline_mode=once),
                pl.BlockSpec((depth, width), lambda t, c: (0, 0), pipeline_mode=once),
            ]
            + [ANY] * len(after),
            out_specs=pl.BlockSpec((tile, width), lambda t, c: (t, 0)),
        ),
        out_shape=jax.ShapeDtypeStruct((n * slab, width), BF16),
        compiler_params=params(),
        cost_estimate=cost,
        name=name,
    )(ids.astype(jnp.int32), basis, basis, *backs, *after)


def on_device(
    gradients,
    left_basis,
    right_basis,
    first_moment,
    second_moment,
    omega_left,
    omega_right,
    sketch_left,
    sketch_right,
):
    n_row, n_col, n_dp = lax.axis_size("row"), lax.axis_size("col"), lax.axis_size("dp")
    row, col, dp = lax.axis_index("row"), lax.axis_index("col"), lax.axis_index("dp")
    y, z_lo, core = col // 4, (col // 2) % 2, col % 2
    n_y = n_col // 4
    own_grad = gradients[0]
    slab, width = own_grad.shape
    rows = slab * n_row
    k_dim = omega_left.shape[1]
    share = rows // n_col
    span = right_basis.shape[1]
    part = slab // n_col
    half = slab // 2

    every = (slice(None), slice(None))
    source_rows = [(row + n_row - s) % n_row for s in (0, 1, 3, 2)]

    came = {0: left_basis}
    for s in (1, 3, 2):
        came[s] = to_row(left_basis, s)
    tops = [own_grad[:half], own_grad[half:]]
    others = [swap_dp(x) for x in tops]

    pieces = []
    for c in range(2):
        for s in range(n_row):
            for z in range(2):
                source, target = (2 * z + c) * share, ((c * n_row + s) * 2 + z) * share
                pieces.append(
                    (came[s], 0, share, slice(source, source + share), slice(target, target + share))
                )
    wide = place(pieces, [jnp.int32(0)] * len(pieces), (share, rows), (others[0],), "left_basis_rows")
    basis = lax.all_gather(wide, "col", axis=0, tiled=True)

    omega_rows = lax.dynamic_slice_in_dim(omega_left, row * slab, slab, 0)
    total_pieces, total_starts = [], []
    probe_left = 0.0
    after = (wide,)
    for h in range(2):
        if h == 0:
            summed = sum_pair(tops[0], others[0], 1.0, after, "sum_replicas_0")
        else:
            summed = sum_replicas(own_grad, tops[1], others[1], omega_rows, after, "sum_replicas_1")
        middle = summed.shape[0] // 2
        before, behind = to_row(summed, 1), to_row(summed, 3)
        after = (before, behind)
        on, back = to_row(before[:middle], 1), to_row(behind[middle:], 3)
        for block, count, i, skip in (
            (summed, half, 0, 0),
            (before, half, 1, 0),
            (behind, half, 2, 0),
            (on, middle, 3, 0),
            (back, half - middle, 3, middle),
        ):
            total_pieces.append((block, 0, count, *every))
            total_starts.append(source_rows[i] * slab + h * half + skip)
            if h == 1 and count != middle:
                probe_left = probe_left + block[count:].astype(F32)
    probe_left = probe_left.astype(BF16)
    right_terms = dot(own_grad, omega_right)

    def by_y(x, axis):
        return jnp.roll(jnp.flip(x, axis), row - (n_y - 1), axis)

    def by_owner(terms):
        terms = terms.astype(BF16).reshape(n_y, 2, 2, part, k_dim).transpose(2, 0, 1, 3, 4)
        return by_y(terms, 1).reshape(n_col, part, k_dim)

    left_terms = dot(own_grad, probe_left, ((1,), (1,)))
    extra = jnp.concatenate([by_owner(right_terms), by_owner(left_terms)], 1)
    extra = jnp.pad(extra, ((0, 0), (0, share - 2 * part), (0, 0))).reshape(-1, k_dim)
    total = place(total_pieces, total_starts, (rows, width), (extra,), "summed_gradient")

    first = (row - y + n_y) % n_y
    left_theirs, sent_b = rotate(
        1 - core, basis, total, right_basis, extra, (), "rotate_theirs_b"
    )
    sent_a = rotate_rest(left_theirs, right_basis, (), "rotate_theirs_a")
    other_b, other_a = swap_core(sent_b), swap_core(sent_a)
    left_mine, mine_b = rotate(core, basis, total, right_basis, extra, (sent_a,), "rotate_mine_b")
    keep_b, sent_b = split_parts(z_lo, mine_b, other_b, n_y, (other_a,), "pair_b")
    came_b = swap_z(sent_b)
    parts_a = rotate_rest_parts(
        first, left_mine, right_basis, other_a, n_y, (keep_b,), "rotate_mine_a"
    )
    came_a = [to_y(parts_a[s], s) for s in (1, 3, 2)]
    parts_b = add_parts(first, keep_b, came_b, n_y, (parts_a[0],), "column_b")
    own_a, sent_a = sum_blocks(z_lo, [parts_a[0]] + came_a, (parts_b[0],), "column_a")
    came_a = swap_z(sent_a)
    own_b = parts_b[0].astype(F32)
    for s in (1, 3, 2):
        own_b = own_b + to_y(parts_b[s], s).astype(F32)
    own_a = own_a + came_a.astype(F32)

    split = BLOCKS_B * BLOCK
    firsts, seconds, directions = [], [], []
    for lower, upper, rotated in ((0, split, own_b[:, :split]), (split, span, own_a)):
        at = slice(lower, upper)
        first_part = 0.9 * first_moment[:, at] + 0.1 * rotated
        second_part = 0.95 * second_moment[:, at] + 0.05 * rotated * rotated
        directions.append((first_part / (jnp.sqrt(second_part) + 1e-08)).astype(BF16))
        firsts.append(first_part)
        seconds.append(second_part)
    first_new = jnp.concatenate(firsts, 1)
    second_new = jnp.concatenate(seconds, 1)
    sketches = own_b[:, split:]

    mine_b = jnp.concatenate([directions[0], sketches.astype(BF16)], 1)
    came_b = [mine_b] + [to_y(mine_b, s) for s in (1, 3, 2)]
    other = swap_z(directions[1])
    mine_a = jnp.where(
        z_lo == 0,
        jnp.concatenate([directions[1], other], 0),
        jnp.concatenate([other, directions[1]], 0),
    )
    came_a = [mine_a] + [to_y(mine_a, s) for s in (1, 3, 2)]
    order = [(first + s) % n_y for s in (0, 1, 3, 2)]
    near_b = place(
        [(x, 0, share, *every) for x in came_b],
        [i * share for i in order],
        (n_y * share, mine_b.shape[1]),
        (mine_a,),
        "direction_near_b",
    )
    far_b = swap_z(near_b)
    pieces = [(x, s * share, share, *every) for x in (near_b, far_b) for s in range(n_y)]
    starts = [2 * s * share + z * share for z in (z_lo, 1 - z_lo) for s in range(n_y)]
    own_b = place(pieces, starts, (2 * n_y * share, mine_b.shape[1]), (), "direction_b")
    own_a = place(
        [(x, 0, 2 * share, *every) for x in came_a],
        [i * 2 * share for i in order],
        (2 * n_y * share, span - split),
        (own_b,),
        "direction_a",
    )
    other_a, other_b = swap_core(own_a), swap_core(own_b)
    probes = [
        by_y(p[:, split:].reshape(n_y, 2, share, k_dim)[:, :, :part], 0) for p in (own_b, other_b)
    ]
    probes = jnp.where(core == 0, jnp.stack(probes, 2), jnp.stack(probes[::-1], 2))
    right_part = probe(own_grad, probes.reshape(slab, k_dim), (own_a,), "right_terms")
    right_came = [to_row(right_part, s) for s in (1, 3, 2)]

    slabs = [(row + s) % n_row for s in range(n_row)]
    far_ids, near_ids = jnp.stack([core] + slabs[1:]), jnp.stack([core] + slabs[:1])
    cut = width * 4 // 7
    sets = ((0, cut), (cut, width))
    backs = [[], []]
    after = (right_part,)
    for part_a, part_b, name in ((own_a, own_b, "own"), (other_a, other_b, "other")):
        for i, (lower, upper) in enumerate(sets):
            if i == 1:
                break
            backs[i].append(
                rotate_back(part_a, part_b, right_basis, lower, upper, after, f"back_{name}_{i}")
            )
            after = (backs[i][-1],)
    kept, sent = sum_blocks(dp, [right_part] + right_came, (backs[0][1],), "right_row_sum")
    kept = kept.astype(BF16)
    right_mine = jnp.where(
        dp == 0, jnp.concatenate([kept, sent], 0), jnp.concatenate([sent, kept], 0)
    )
    far_0 = update_rows(far_ids, basis, backs[0], slab, CHEAP, (sent,), "update_far_0")
    came_0 = [to_row(far_0[(s - 1) * slab : s * slab], s) for s in (2, 1, 3)]
    backs[1].append(
        rotate_back(own_a, own_b, right_basis, *sets[1], (far_0,), "back_own_1")
    )
    backs[1].append(
        rotate_back(other_a, other_b, right_basis, *sets[1], (backs[1][0],), "back_other_1")
    )
    far_1 = update_rows(far_ids, basis, backs[1], slab, CHEAP, (), "update_far_1")
    came_1 = [to_row(far_1[(s - 1) * slab : s * slab], s) for s in (2, 1, 3)]
    near_0 = update_rows(near_ids, basis, backs[0], slab, CHEAP, (far_1,), "update_near_0")

    own_0, sent = sum_blocks(dp, [near_0] + came_0, (), "update_sum_0")
    update_0 = (own_0 + swap_dp(sent).astype(F32)).astype(BF16)
    near_1 = update_rows(near_ids, basis, backs[1], slab, HEAVY, (sent,), "update_near_1")
    own_1, sent = sum_blocks(dp, [near_1] + came_1, (), "update_sum_1")
    update_1 = (own_1 + swap_dp(sent).astype(F32)).astype(BF16)
    update = jnp.concatenate([update_0, update_1], 1)

    right_sum = sum_pair(right_mine, swap_dp(right_mine), 1.0, (near_1,), "right_sum").astype(F32)
    right_new = 0.5 * sketch_right + 0.5 * right_sum / (n_dp * math.sqrt(rows))

    lines = part // n_dp
    left_mine = lax.dynamic_slice_in_dim(sketches, part + dp * lines, lines, 0)
    left_sent = lax.dynamic_slice_in_dim(sketches, part + (1 - dp) * lines, lines, 0)
    left_sent = jnp.pad(left_sent, ((0, 32 - lines), (0, 0))).astype(BF16)
    left_sent = sum_pair(left_sent, left_sent, 0.5, (near_1,), "left_sent")
    left_sum = left_mine + swap_dp(left_sent)[:lines].astype(F32)
    f_dim = width * n_col
    left_new = 0.5 * sketch_left + 0.5 * left_sum / (n_dp * math.sqrt(f_dim))

    return (
        update,
        first_new,
        second_new,
        left_new,
        right_new,
    )


def solution(mesh):
    return jax.shard_map(
        on_device,
        mesh=mesh,
        in_specs=(
            P("dp", "row", "col"),
            P("col", "row"),
            P("col", ("row", "dp")),
            P("col", ("row", "dp")),
            P("col", ("row", "dp")),
            P(),
            P("col", None),
            P(("row", "col", "dp"), None),
            P("col", None),
        ),
        out_specs=(
            P(("row", "dp"), "col"),
            P("col", ("row", "dp")),
            P("col", ("row", "dp")),
            P(("row", "col", "dp"), None),
            P("col", None),
        ),
        check_vma=False,
    )
```
